128 devices in a mesh: var: 8 (over z_lo, y), lon: 16 (over x, z_hi, core).
Axes of the slice: x: 4, y: 4, z: 4 (z_hi: 2, z_lo: 2; z = z_hi * 2 + z_lo), core: 2. Of those that a mesh axis runs over, the one named last changes fastest.
Arguments:
- pixels: bfloat16 [8, 5, 16, 16384], P('var', None, None, 'lon'), may hold values from -6 to 6
- w_embed: bfloat16 [80, 512], replicated, may hold values from -0.625 to 0.625
- level_embed: bfloat16 [8, 512], replicated, may hold values from -6 to 6
- latents: bfloat16 [3, 512], replicated, may hold values from -96 to 96
- w_query: bfloat16 [512, 1024], replicated, may hold values from -0.25 to 0.25
- w_key: bfloat16 [512, 1024], replicated, may hold values from -0.25 to 0.25
- w_value: bfloat16 [512, 1024], replicated, may hold values from -0.25 to 0.25
- w_out: bfloat16 [1024, 512], replicated, may hold values from -0.1875 to 0.1875
- w_up: bfloat16 [512, 2048], replicated, may hold values from -0.25 to 0.25
- w_down: bfloat16 [2048, 512], replicated, may hold values from -0.125 to 0.125
- cotangent: bfloat16 [3, 16384, 512], P(None, ('lon', 'var')), may hold values from -0.02734375 to 0.02734375
Outputs:
- pooled: bfloat16 [3, 16384, 512], P(None, ('lon', 'var'))
- grad_embed: float32 [80, 512], replicated
- grad_level: float32 [8, 512], replicated
- grad_latents: float32 [3, 512], replicated
- grad_query: float32 [512, 1024], replicated
- grad_key: float32 [512, 1024], replicated
- grad_value: float32 [512, 1024], replicated
- grad_out: float32 [1024, 512], replicated
- grad_up: float32 [512, 2048], P(None, 'lon')
- grad_down: float32 [2048, 512], P('lon')
The draws below stay inside these ranges and needn't reach their ends.
All inputs are finite; a program needn't handle non-finite values.
Results may differ from the reference program's by a relative error of at most 0.024.
The reference program's roundings to bfloat16 on the way count: a program that leaves them out, or rounds other values in their place, can miss the bound.
Values may be sent and summed in bfloat16 or wider, within the bound.
A program may use at most 128 MiB of HBM per device.

```python
import math
import jax
import jax.numpy as jnp
from jax import lax

D = 512
FF = 2048
HEADS = 16
VARS = 5
PP = 16
LAT = 3
LEV = 8
PATCH_LON = 1024
NPATCH = 16384
ATT = 1024
N_VAR = 8


def draw_latents(key, part):
    key = jax.random.fold_in(key, 7)
    values = jax.random.truncated_normal(key, -4.0, 4.0, (LAT, D), jnp.float32)
    return values.astype(jnp.bfloat16)


def block_scale(rng, extent, cuts, smallest, high):
    gain, own = 1.0, jax.random.fold_in(rng, 6)
    for dim, parts in cuts:
        heights = jnp.exp(jax.random.uniform(jax.random.fold_in(own, dim), (parts,), jnp.float32, smallest / len(cuts), high / len(cuts)))
        gain = gain * jnp.repeat(heights, extent[dim] // parts).reshape([-1 if axis == dim else 1 for axis in range(len(extent))])
    return gain


def centred(own_key, shape, scale, reach, shards=(), kind=jnp.bfloat16):
    array = jax.random.normal(own_key, shape, jnp.float32) * scale
    if len(shards) > 0:
        array = block_scale(own_key, shape, shards, -0.22, 0.18) * array
    return jnp.clip(array, min=-reach, max=reach).astype(kind)


def setup_inputs(seed: int = 0) -> dict:
    key_list = jax.random.split(jax.random.key(seed), 12)
    return {
        "pixels": centred(key_list[0], (LEV, VARS, PP, NPATCH), 1.0, 6.0, ((0, 8), (3, 16))),
        "w_embed": centred(key_list[1], (VARS * PP, D), (VARS * PP) ** -0.5, 0.625),
        "level_embed": centred(key_list[2], (LEV, D), 1.0, 6.0),
        "latents": draw_latents(jax.random.fold_in(key_list[11], 71), 0),
        "w_query": centred(key_list[4], (D, ATT), D ** -0.5, 0.25),
        "w_key": centred(key_list[5], (D, ATT), D ** -0.5, 0.25),
        "w_value": centred(key_list[6], (D, ATT), D ** -0.5, 0.25),
        "w_out": centred(key_list[7], (ATT, D), ATT ** -0.5, 0.1875),
        "w_up": centred(key_list[8], (D, FF), D ** -0.5, 0.25),
        "w_down": centred(key_list[9], (FF, D), FF ** -0.5, 0.125),
        "cotangent": centred(key_list[10], (LAT, NPATCH, D), (LAT * NPATCH) ** -0.5, 0.02734375, ((1, 128),)),
    }


F32 = jnp.float32
BF16 = jnp.bfloat16
EPSILON = 1e-05

def contract(form, left, right):
    return jnp.einsum(form, left.astype(F32), right.astype(F32))

def flat_outer(left, right):
    left_rows = left.reshape(-1, left.shape[-1])
    right_rows = right.reshape(-1, right.shape[-1])
    return lax.dot_general(left_rows, right_rows, (((0,), (0,)), ((), ())), preferred_element_type=F32)

def times_transposed(left, weight):
    return lax.dot_general(left, weight, (((left.ndim - 1,), (1,)), ((), ())), preferred_element_type=F32)

def embed_levels(pixels, w_embed, level_rows):
    levels, variables, pixel_count, patches = pixels.shape
    folded = pixels.reshape(levels, variables * pixel_count, patches)
    summed = lax.dot_general(folded, w_embed, (((1,), (0,)), ((), ())), preferred_element_type=F32)
    return (summed + level_rows.astype(F32)[:, None, :]).astype(BF16)

def embed_grads(pixels, d_tokens):
    levels, variables, pixel_count, patches = pixels.shape
    folded = pixels.reshape(levels, variables * pixel_count, patches)
    grad_embed = lax.dot_general(folded, d_tokens, (((0, 2), (0, 1)), ((), ())), preferred_element_type=F32)
    return (grad_embed, lax.optimization_barrier(jnp.sum(d_tokens.astype(F32), axis=1)))

def front(tokens, latents, w_query, w_key, w_value, w_out, w_up, w_down, cotangent):
    levels, patches, width = tokens.shape
    n_lat = latents.shape[0]
    inner = w_key.shape[1]
    head_dim = inner // HEADS
    scale = 1.0 / math.sqrt(head_dim)
    whole = tokens.astype(F32)
    center = whole - lax.optimization_barrier(jnp.mean(whole, axis=-1, keepdims=True))
    inverse = lax.rsqrt(lax.optimization_barrier(jnp.mean(center * center, axis=-1, keepdims=True)) + EPSILON)
    unit = center * inverse
    normed = unit.astype(BF16)
    keys = jnp.dot(normed, w_key, preferred_element_type=F32).astype(BF16)
    values = jnp.dot(normed, w_value, preferred_element_type=F32).astype(BF16)
    queries = jnp.dot(latents, w_query, preferred_element_type=F32).astype(BF16)
    key_heads = keys.reshape(levels, patches, HEADS, head_dim)
    value_heads = values.reshape(levels, patches, HEADS, head_dim)
    query_heads = queries.reshape(n_lat, HEADS, head_dim)
    scores = contract('qhj,lphj->hqlp', query_heads, key_heads) * scale
    highest = lax.optimization_barrier(jnp.max(scores, axis=2, keepdims=True))
    expo = jnp.exp(scores - highest)
    probs = expo / lax.optimization_barrier(jnp.sum(expo, axis=2, keepdims=True))
    weights = probs.astype(BF16)
    mixed = contract('hqlp,lphj->qphj', weights, value_heads).astype(BF16).reshape(n_lat, patches, inner)
    attended = (latents.astype(F32)[:, None, :] + jnp.dot(mixed, w_out, preferred_element_type=F32)).astype(BF16)
    pre_act = jnp.dot(attended, w_up, preferred_element_type=F32)
    hidden = jax.nn.gelu(pre_act).astype(BF16)
    pooled = (attended.astype(F32) + jnp.dot(hidden, w_down, preferred_element_type=F32)).astype(BF16)
    grad_down = flat_outer(hidden, cotangent)
    d_hidden = times_transposed(cotangent, w_down)
    d_pre = jax.vjp(jax.nn.gelu, pre_act)[1](d_hidden)[0].astype(BF16)
    grad_up = flat_outer(attended, d_pre)
    d_att = cotangent.astype(F32) + times_transposed(d_pre, w_up)
    d_att_b = d_att.astype(BF16)
    grad_out = flat_outer(mixed, d_att_b)
    saved = (unit, inverse, normed, key_heads, value_heads, query_heads, probs, weights, d_att, d_att_b)
    return (pooled, (grad_out, grad_up, grad_down), saved)

def back(saved, latents, w_query, w_key, w_value, w_out):
    unit, inverse, normed, key_heads, value_heads, query_heads, probs, weights, d_att, d_att_b = saved
    levels, patches, heads, head_dim = key_heads.shape
    n_lat = query_heads.shape[0]
    inner = heads * head_dim
    scale = 1.0 / math.sqrt(head_dim)
    d_mixed = times_transposed(d_att_b, w_out).astype(BF16).reshape(n_lat, patches, heads, head_dim)
    d_weights = contract('qphj,lphj->hqlp', d_mixed, value_heads)
    d_values = contract('hqlp,qphj->lphj', weights, d_mixed).astype(BF16).reshape(levels, patches, inner)
    d_scores = (probs * (d_weights - lax.optimization_barrier(jnp.sum(probs * d_weights, axis=2, keepdims=True))) * scale).astype(BF16)
    d_queries = contract('hqlp,lphj->qhj', d_scores, key_heads).reshape(n_lat, inner)
    d_keys = contract('hqlp,qhj->lphj', d_scores, query_heads).astype(BF16).reshape(levels, patches, inner)
    grad_key = flat_outer(normed, d_keys)
    grad_value = flat_outer(normed, d_values)
    d_normed = times_transposed(d_keys, w_key) + times_transposed(d_values, w_value)
    d_tokens = (inverse * (d_normed - lax.optimization_barrier(jnp.mean(d_normed, axis=-1, keepdims=True)) - unit * lax.optimization_barrier(jnp.mean(d_normed * unit, axis=-1, keepdims=True)))).astype(BF16)
    grad_query = lax.dot_general(latents.astype(F32), d_queries, (((0,), (0,)), ((), ())), precision=lax.Precision.HIGHEST)
    grad_lat = lax.optimization_barrier(jnp.sum(d_att, axis=1)) + lax.dot_general(d_queries, w_query.astype(F32), (((1,), (1,)), ((), ())), precision=lax.Precision.HIGHEST)
    return (d_tokens, (grad_query, grad_key, grad_value, grad_lat))

def reference(pixels, w_embed, level_embed, latents, w_query, w_key, w_value, w_out, w_up, w_down, cotangent):
    npatch = pixels.shape[3]
    block = PATCH_LON // N_VAR
    count = npatch // block
    width = w_embed.shape[1]
    inner = w_key.shape[1]
    ffn = w_up.shape[1]
    start_grads = (jnp.zeros(w_embed.shape, F32), jnp.zeros(level_embed.shape, F32), jnp.zeros(latents.shape, F32), jnp.zeros((width, inner), F32), jnp.zeros((width, inner), F32), jnp.zeros((width, inner), F32), jnp.zeros((inner, width), F32), jnp.zeros((width, ffn), F32), jnp.zeros((ffn, width), F32))

    def step(carry, index):
        start = (index * block).astype(jnp.int32)
        piece = lax.dynamic_slice_in_dim(pixels, start, block, 3)
        cot_piece = lax.dynamic_slice_in_dim(cotangent, start, block, 1)
        tokens = embed_levels(piece, w_embed, level_embed)
        pooled, mlp_grads, saved = front(tokens, latents, w_query, w_key, w_value, w_out, w_up, w_down, cot_piece)
        d_tokens, attn_grads = back(saved, latents, w_query, w_key, w_value, w_out)
        grad_embed, grad_level = embed_grads(piece, d_tokens)
        grad_query, grad_key, grad_value, grad_lat = attn_grads
        grad_out, grad_up, grad_down = mlp_grads
        fresh = (grad_embed, grad_level, grad_lat, grad_query, grad_key, grad_value, grad_out, grad_up, grad_down)
        return (tuple((old + new for old, new in zip(carry, fresh))), pooled)
    totals, blocks = lax.scan(step, start_grads, jnp.arange(count, dtype=jnp.int32))
    pooled = jnp.transpose(blocks, (1, 0, 2, 3)).reshape(latents.shape[0], npatch, width)
    return (pooled, totals[0], totals[1], totals[2], totals[3], totals[4], totals[5], totals[6], totals[7], totals[8])
```

```python
import functools
import math

import jax
import jax.numpy as jnp
from jax import lax
from jax.experimental import pallas as pl
from jax.experimental.pallas import tpu as pltpu
from jax.sharding import PartitionSpec as P

F32 = jnp.float32
BF16 = jnp.bfloat16
EPSILON = 1e-05
HEADS = 16
HEAD = 64
LEV = 8
LAT = 3
ROWS = 128
TILE = 256
PAD = 128
SMALL = 192
GELU_C = math.sqrt(2.0 / math.pi)
GELU_A = 0.044715


def mm(left, right):
    return lax.dot_general(left, right, (((1,), (0,)), ((), ())), preferred_element_type=F32)


def mm_nt(left, right):
    return lax.dot_general(left, right, (((1,), (1,)), ((), ())), preferred_element_type=F32)


def mm_tn(left, right):
    return lax.dot_general(left, right, (((0,), (0,)), ((), ())), preferred_element_type=F32)


def split(value):
    high = value.astype(BF16)
    return high, (value - high.astype(F32)).astype(BF16)


def head_rows(inner):
    row = lax.broadcasted_iota(jnp.int32, (PAD, inner), 0)
    head = lax.broadcasted_iota(jnp.int32, (PAD, inner), 1) // HEAD
    return row, head


def query_rows(latents, w_query):
    queries = mm(latents, w_query).astype(BF16).astype(F32)
    inner = queries.shape[1]
    row, head = head_rows(inner)
    spread = jnp.zeros((PAD, inner), F32)
    for q in range(LAT):
        spread = jnp.where(row == q * HEADS + head, queries[q : q + 1, :], spread)
    return spread.astype(BF16)


def prepare(latents, w_query, w_key, select, wq_high, wq_low):
    inner = w_key.shape[1]
    row, head = head_rows(inner)
    for q in range(LAT):
        select[q] = jnp.where(row == q * HEADS + head, 1.0, 0.0).astype(BF16)
    folded = mm_nt(query_rows(latents[...], w_query[...]), w_key[...])
    high, low = split(folded)
    wq_high[...] = high
    wq_low[...] = low


def forward(
    px, w_embed, level_embed, w_value, wq_high, wq_low, level_rows, unit, inv, normed, normed_t, values, scores
):
    level_rows[...] = level_embed[...].astype(F32)

    @pl.loop(0, LEV)
    def _(l):
        token = mm_tn(px[l], w_embed[...]) + level_rows[pl.ds(l, 1), :]
        token = token.astype(BF16).astype(F32)
        center = token - jnp.mean(token, axis=-1, keepdims=True)
        inverse = lax.rsqrt(jnp.mean(center * center, axis=-1, keepdims=True) + EPSILON)
        own = center * inverse
        unit[l] = own
        inv[l] = jnp.broadcast_to(inverse, (ROWS, PAD))
        own = own.astype(BF16)
        normed[pl.ds(pl.multiple_of(l * ROWS, ROWS), ROWS), :] = own
        scores[l] = (mm_nt(own, wq_high[...]) + mm_nt(own, wq_low[...])) * (1.0 / math.sqrt(HEAD))
        values[l] = mm(own, w_value[...]).astype(BF16)

    normed_t[...] = normed[...].T


def softmax(scores, weights):
    highest = scores[0]
    for l in range(1, LEV):
        highest = jnp.maximum(highest, scores[l])
    total = jnp.zeros_like(highest)
    for l in range(LEV):
        expo = jnp.exp(scores[l] - highest)
        scores[l] = expo
        total = total + expo
    for l in range(LEV):
        prob = scores[l] / total
        scores[l] = prob
        weights[l * ROWS : (l + 1) * ROWS, :] = prob.astype(BF16)


def mix(weights, select, values, spread, mixed):
    inner = values.shape[2]

    @pl.loop(0, inner // TILE)
    def _(t):
        cols = pl.ds(pl.multiple_of(t * TILE, TILE), TILE)
        for q in range(LAT):
            total = jnp.zeros((ROWS, TILE), F32)
            for l in range(LEV):
                own = mm(weights[l * ROWS : (l + 1) * ROWS, :], select[q, :, cols])
                spread[q, l, :, cols] = own.astype(BF16)
                total = total + own * values[l, :, cols].astype(F32)
            mixed[q * ROWS : (q + 1) * ROWS, cols] = total.astype(BF16)


def attend(latents, mixed, w_out, attended):
    for q in range(LAT):
        rows = slice(q * ROWS, (q + 1) * ROWS)
        own = mm(mixed[rows, :], w_out[...]) + latents[q : q + 1, :].astype(F32)
        attended[rows, :] = own.astype(BF16)


def feed_forward(attended, cot, w_up, w_down, pool_sum, d_att, put_up, put_down):
    pool_sum[...] = attended[...].astype(F32)
    d_att[...] = cot[...].astype(F32)

    @pl.loop(0, w_up.shape[1] // TILE)
    def _(t):
        cols = pl.ds(pl.multiple_of(t * TILE, TILE), TILE)
        pre = mm(attended[...], w_up[:, cols])
        square = pre * pre
        bent = jnp.tanh(GELU_C * (pre + GELU_A * (square * pre)))
        half = 0.5 * (1.0 + bent)
        hidden = (pre * half).astype(BF16)
        slope = half + 0.5 * pre * (1.0 - bent * bent) * (GELU_C * (1.0 + 3.0 * GELU_A * square))
        d_pre = (mm_nt(cot[...], w_down[cols, :]) * slope).astype(BF16)
        pool_sum[...] += mm(hidden, w_down[cols, :])
        d_att[...] += mm_nt(d_pre, w_up[:, cols])
        put_down(t, mm_tn(hidden, cot[...]).astype(BF16))
        put_up(t, mm_tn(d_pre, attended[...]).astype(BF16))


def value_back(spread, d_mixed, values, normed_t, select, d_values, d_weights, put_value):
    inner = values.shape[2]
    d_weights[...] = jnp.zeros_like(d_weights)

    @pl.loop(0, inner // TILE)
    def _(t):
        cols = pl.ds(pl.multiple_of(t * TILE, TILE), TILE)
        for l in range(LEV):
            rows = slice(l * ROWS, (l + 1) * ROWS)
            own = values[l, :, cols].astype(F32)
            total = jnp.zeros((ROWS, TILE), F32)
            back = jnp.zeros((ROWS, PAD), F32)
            for q in range(LAT):
                d_mix = d_mixed[q * ROWS : (q + 1) * ROWS, cols].astype(F32)
                total = total + spread[q, l, :, cols].astype(F32) * d_mix
                back = back + mm_nt((d_mix * own).astype(BF16), select[q, :, cols])
            d_values[rows, cols] = total.astype(BF16)
            d_weights[rows, :] += back
        put_value(t, mm(normed_t[...], d_values[:, cols]).astype(BF16))


def score_back(probs, d_weights, d_scores):
    total = jnp.zeros((ROWS, PAD), F32)
    for l in range(LEV):
        total = total + probs[l] * d_weights[l * ROWS : (l + 1) * ROWS, :]
    for l in range(LEV):
        rows = slice(l * ROWS, (l + 1) * ROWS)
        own = probs[l] * (d_weights[rows, :] - total) * (1.0 / math.sqrt(HEAD))
        d_scores[rows, :] = own.astype(BF16)


def token_back(px, unit, inv, w_value, wq_high, d_values, d_scores, small):
    small[48:SMALL, :] = jnp.zeros((SMALL - 48, small.shape[1]), F32)

    @pl.loop(0, LEV)
    def _(l):
        rows = pl.ds(pl.multiple_of(l * ROWS, ROWS), ROWS)
        d_normed = mm_nt(d_values[rows, :], w_value[...]) + mm(d_scores[rows, :], wq_high[...])
        own = unit[l]
        inverse = inv[l][:, :1]
        d_token = inverse * (
            d_normed
            - jnp.mean(d_normed, axis=-1, keepdims=True)
            - own * jnp.mean(d_normed * own, axis=-1, keepdims=True)
        )
        d_token = d_token.astype(BF16)
        small[48:128, :] += mm(px[l], d_token)
        small[pl.ds(128 + l, 1), :] = jnp.sum(d_token.astype(F32), axis=0, keepdims=True)


def local_kernel(
    px, w_embed, level_embed, latents, w_query, w_key, w_value, w_out, w_up, w_down, cot,
    pooled, up_all, down_all, out_all, value_all, small,
    select, wq_high, wq_low, level_rows, unit, inv, normed, normed_t, values, scores, weights, spread, mixed,
    attended, pool_sum, d_att, d_att_b, d_mixed, d_values, d_weights, d_scores,
):
    prepare(latents, w_query, w_key, select, wq_high, wq_low)
    forward(
        px, w_embed, level_embed, w_value, wq_high, wq_low, level_rows, unit, inv, normed, normed_t, values, scores
    )
    softmax(scores, weights)
    mix(weights, select, values, spread, mixed)
    attend(latents, mixed, w_out, attended)

    def put_up(t, block):
        up_all[pl.ds(pl.multiple_of(t * TILE, TILE), TILE), :] = block

    def put_down(t, block):
        down_all[pl.ds(pl.multiple_of(t * TILE, TILE), TILE), :] = block

    def put_value(t, block):
        value_all[t] = block

    feed_forward(attended, cot, w_up, w_down, pool_sum, d_att, put_up, put_down)
    pooled[...] = pool_sum[...].astype(BF16)
    d_att_b[...] = d_att[...].astype(BF16)
    d_mixed[...] = mm_nt(d_att_b[...], w_out[...]).astype(BF16)
    for half in range(2):
        out_all[half] = mm_tn(mixed[...], d_att_b[:, half * TILE : (half + 1) * TILE]).astype(BF16)
    value_back(spread, d_mixed, values, normed_t, select, d_values, d_weights, put_value)
    score_back(scores, d_weights, d_scores)
    token_back(px, unit, inv, w_value, wq_high, d_values, d_scores, small)
    small[0:48, :] = mm_tn(d_scores[...], normed[...])[0:48, :]
    for q in range(LAT):
        small[136 + q : 137 + q, :] = jnp.sum(d_att[q * ROWS : (q + 1) * ROWS, :], axis=0, keepdims=True)


def local_part(px, w_embed, level_embed, latents, w_query, w_key, w_value, w_out, w_up, w_down, cot):
    width, inner, ffn = w_key.shape[0], w_key.shape[1], w_up.shape[1]
    every, pairs = LEV * ROWS, LAT * ROWS
    shape = jax.ShapeDtypeStruct
    whole = pl.BlockSpec(memory_space=pltpu.VMEM)
    return pl.pallas_call(
        local_kernel,
        out_shape=(
            shape((pairs, width), BF16),
            shape((ffn, width), BF16),
            shape((ffn, width), BF16),
            shape((2, inner, TILE), BF16),
            shape((4, width, TILE), BF16),
            shape((SMALL, width), F32),
        ),
        in_specs=[whole] * 11,
        out_specs=(whole,) * 6,
        scratch_shapes=[
            pltpu.VMEM((LAT, PAD, inner), BF16),
            pltpu.VMEM((PAD, width), BF16),
            pltpu.VMEM((PAD, width), BF16),
            pltpu.VMEM((LEV, width), F32),
            pltpu.VMEM((LEV, ROWS, width), F32),
            pltpu.VMEM((LEV, ROWS, PAD), F32),
            pltpu.VMEM((every, width), BF16),
            pltpu.VMEM((width, every), BF16),
            pltpu.VMEM((LEV, ROWS, inner), BF16),
            pltpu.VMEM((LEV, ROWS, PAD), F32),
            pltpu.VMEM((every, PAD), BF16),
            pltpu.VMEM((LAT, LEV, ROWS, inner), BF16),
            pltpu.VMEM((pairs, inner), BF16),
            pltpu.VMEM((pairs, width), BF16),
            pltpu.VMEM((pairs, width), F32),
            pltpu.VMEM((pairs, width), F32),
            pltpu.VMEM((pairs, width), BF16),
            pltpu.VMEM((pairs, inner), BF16),
            pltpu.VMEM((every, inner), BF16),
            pltpu.VMEM((every, PAD), F32),
            pltpu.VMEM((every, PAD), BF16),
        ],
        compiler_params=pltpu.CompilerParams(vmem_limit_bytes=60 * 1024 * 1024),
        name="local_part",
    )(px, w_embed, level_embed, latents, w_query, w_key, w_value, w_out, w_up, w_down, cot)


def finish_kernel(
    small, value_all, out_all, latents, w_query, w_key,
    grad_embed, grad_level, grad_lat, grad_query, grad_key, grad_value, grad_out,
):
    grad_embed[...] = small[48:128, :].astype(F32)
    grad_level[...] = small[128:136, :].astype(F32)
    for t in range(4):
        grad_value[:, t * TILE : (t + 1) * TILE] = value_all[t].astype(F32)
    for half in range(2):
        grad_out[:, half * TILE : (half + 1) * TILE] = out_all[half].astype(F32)
    rows = query_rows(latents[...], w_query[...])
    high, low = split(small[0:48, :].astype(F32))
    grad_key[...] = mm_tn(high, rows[0:48, :]) + mm_tn(low, rows[0:48, :])
    spread = mm(high, w_key[...]) + mm(low, w_key[...])
    inner = w_key.shape[1]
    row = lax.broadcasted_iota(jnp.int32, (48, inner), 0)
    head = lax.broadcasted_iota(jnp.int32, (48, inner), 1) // HEAD
    own = []
    for q in range(LAT):
        own.append(jnp.sum(jnp.where(row == q * HEADS + head, spread, 0.0), axis=0, keepdims=True))
    d_queries = jnp.concatenate(own, axis=0)
    high, low = split(d_queries)
    grad_query[...] = mm_tn(latents[...], high) + mm_tn(latents[...], low)
    grad_lat[...] = small[136:139, :].astype(F32) + mm_nt(high, w_query[...]) + mm_nt(low, w_query[...])


def finish(small, value_all, out_all, latents, w_query, w_key):
    width, inner = w_key.shape
    shape = jax.ShapeDtypeStruct
    whole = pl.BlockSpec(memory_space=pltpu.VMEM)
    return pl.pallas_call(
        finish_kernel,
        out_shape=(
            shape((80, width), F32),
            shape((LEV, width), F32),
            shape((LAT, width), F32),
            shape((width, inner), F32),
            shape((width, inner), F32),
            shape((width, inner), F32),
            shape((inner, width), F32),
        ),
        in_specs=[whole] * 6,
        out_specs=(whole,) * 7,
        compiler_params=pltpu.CompilerParams(vmem_limit_bytes=60 * 1024 * 1024),
        name="finish",
    )(small, value_all, out_all, latents, w_query, w_key)


def on_device(
    pixels, w_embed, level_embed, latents, w_query, w_key, w_value, w_out, w_up, w_down, cotangent
):
    width = w_embed.shape[1]
    own = pixels.reshape(80, LEV, ROWS)
    px = lax.all_to_all(own, "var", split_axis=1, concat_axis=1, tiled=True)
    px = jnp.transpose(px, (1, 0, 2))
    pooled, up_all, down_all, out_all, value_all, small = local_part(
        px, w_embed, level_embed, latents, w_query, w_key, w_value, w_out, w_up, w_down,
        cotangent.reshape(LAT * ROWS, width),
    )
    both = jnp.concatenate(
        [up_all.reshape(16, -1, width), down_all.reshape(16, -1, width)], axis=1
    )
    part = lax.psum_scatter(both, "lon", scatter_dimension=0, tiled=True)
    part = lax.psum(part, "var")[0].astype(F32)
    up_part, down_part = part[:ROWS], part[ROWS:]
    small, value_all, out_all = lax.psum((small.astype(BF16), value_all, out_all), ("var", "lon"))
    grads = finish(small, value_all, out_all, latents, w_query, w_key)
    return (pooled.reshape(LAT, ROWS, width), *grads, jnp.transpose(up_part), down_part)


def solution(mesh):
    return jax.shard_map(
        on_device,
        mesh=mesh,
        in_specs=(
            P("var", None, None, "lon"),
            *([P()] * 9),
            P(None, ("lon", "var"), None),
        ),
        out_specs=(
            P(None, ("lon", "var"), None),
            *([P()] * 7),
            P(None, "lon"),
            P("lon", None),
        ),
        check_vma=False,
    )
```

```python
import functools
import math

import jax
import jax.numpy as jnp
from jax import lax
from jax.experimental import pallas as pl
from jax.experimental.pallas import tpu as pltpu
from jax.sharding import PartitionSpec as P

F32 = jnp.float32
BF16 = jnp.bfloat16
EPSILON = 1e-05
HEADS = 16
HEAD = 64
LEV = 8
LAT = 3
ROWS = 128
TILE = 256
PAD = 128
SMALL = 192
GELU_C = math.sqrt(2.0 / math.pi)
GELU_A = 0.044715


def mm(left, right):
    return lax.dot_general(left, right, (((1,), (0,)), ((), ())), preferred_element_type=F32)


def mm_nt(left, right):
    return lax.dot_general(left, right, (((1,), (1,)), ((), ())), preferred_element_type=F32)


def mm_tn(left, right):
    return lax.dot_general(left, right, (((0,), (0,)), ((), ())), preferred_element_type=F32)


def split(value):
    high = value.astype(BF16)
    return high, (value - high.astype(F32)).astype(BF16)


def head_rows(inner):
    row = lax.broadcasted_iota(jnp.int32, (PAD, inner), 0)
    head = lax.broadcasted_iota(jnp.int32, (PAD, inner), 1) // HEAD
    return row, head


def query_rows(latents, w_query):
    queries = mm(latents, w_query).astype(BF16).astype(F32)
    inner = queries.shape[1]
    row, head = head_rows(inner)
    spread = jnp.zeros((PAD, inner), F32)
    for q in range(LAT):
        spread = jnp.where(row == q * HEADS + head, queries[q : q + 1, :], spread)
    return spread.astype(BF16)


def prepare(latents, w_query, w_key, select, wq_high, wq_low):
    inner = w_key.shape[1]
    row, head = head_rows(inner)
    for q in range(LAT):
        select[q] = jnp.where(row == q * HEADS + head, 1.0, 0.0).astype(BF16)
    folded = mm_nt(query_rows(latents[...], w_query[...]), w_key[...])
    high, low = split(folded)
    wq_high[...] = high
    wq_low[...] = low


def forward(
    px, w_embed, level_embed, w_value, wq_high, wq_low, level_rows, unit, inv, normed, normed_t, values, scores
):
    level_rows[...] = level_embed[...].astype(F32)

    @pl.loop(0, LEV)
    def _(l):
        token = mm_tn(px[l], w_embed[...]) + level_rows[pl.ds(l, 1), :]
        token = token.astype(BF16).astype(F32)
        center = token - jnp.mean(token, axis=-1, keepdims=True)
        inverse = lax.rsqrt(jnp.mean(center * center, axis=-1, keepdims=True) + EPSILON)
        own = center * inverse
        unit[l] = own
        inv[l] = jnp.broadcast_to(inverse, (ROWS, PAD))
        own = own.astype(BF16)
        normed[pl.ds(pl.multiple_of(l * ROWS, ROWS), ROWS), :] = own
        scores[l] = (mm_nt(own, wq_high[...]) + mm_nt(own, wq_low[...])) * (1.0 / math.sqrt(HEAD))
        values[l] = mm(own, w_value[...]).astype(BF16)

    normed_t[...] = normed[...].T


def softmax(scores, weights):
    highest = scores[0]
    for l in range(1, LEV):
        highest = jnp.maximum(highest, scores[l])
    total = jnp.zeros_like(highest)
    for l in range(LEV):
        expo = jnp.exp(scores[l] - highest)
        scores[l] = expo
        total = total + expo
    for l in range(LEV):
        prob = scores[l] / total
        scores[l] = prob
        weights[l * ROWS : (l + 1) * ROWS, :] = prob.astype(BF16)


def mix(weights, select, values, spread, mixed):
    inner = values.shape[2]

    @pl.loop(0, inner // TILE)
    def _(t):
        cols = pl.ds(pl.multiple_of(t * TILE, TILE), TILE)
        for q in range(LAT):
            total = jnp.zeros((ROWS, TILE), F32)
            for l in range(LEV):
                own = mm(weights[l * ROWS : (l + 1) * ROWS, :], select[q, :, cols])
                spread[q, l, :, cols] = own.astype(BF16)
                total = total + own * values[l, :, cols].astype(F32)
            mixed[q * ROWS : (q + 1) * ROWS, cols] = total.astype(BF16)


def attend(latents, mixed, w_out, attended):
    for q in range(LAT):
        rows = slice(q * ROWS, (q + 1) * ROWS)
        own = mm(mixed[rows, :], w_out[...]) + latents[q : q + 1, :].astype(F32)
        attended[rows, :] = own.astype(BF16)


def feed_forward(attended, cot, w_up, w_down, pool_sum, d_att, put_up, put_down):
    pool_sum[...] = attended[...].astype(F32)
    d_att[...] = cot[...].astype(F32)

    @pl.loop(0, w_up.shape[1] // TILE)
    def _(t):
        cols = pl.ds(pl.multiple_of(t * TILE, TILE), TILE)
        pre = mm(attended[...], w_up[:, cols])
        square = pre * pre
        bent = jnp.tanh(GELU_C * (pre + GELU_A * (square * pre)))
        half = 0.5 * (1.0 + bent)
        hidden = (pre * half).astype(BF16)
        slope = half + 0.5 * pre * (1.0 - bent * bent) * (GELU_C * (1.0 + 3.0 * GELU_A * square))
        d_pre = (mm_nt(cot[...], w_down[cols, :]) * slope).astype(BF16)
        pool_sum[...] += mm(hidden, w_down[cols, :])
        d_att[...] += mm_nt(d_pre, w_up[:, cols])
        put_down(t, mm_tn(hidden, cot[...]).astype(BF16))
        put_up(t, mm_tn(d_pre, attended[...]).astype(BF16))


def value_back(spread, d_mixed, values, normed_t, select, d_values, d_weights, put_value):
    inner = values.shape[2]
    d_weights[...] = jnp.zeros_like(d_weights)

    @pl.loop(0, inner // TILE)
    def _(t):
        cols = pl.ds(pl.multiple_of(t * TILE, TILE), TILE)
        for l in range(LEV):
            rows = slice(l * ROWS, (l + 1) * ROWS)
            own = values[l, :, cols].astype(F32)
            total = jnp.zeros((ROWS, TILE), F32)
            back = jnp.zeros((ROWS, PAD), F32)
            for q in range(LAT):
                d_mix = d_mixed[q * ROWS : (q + 1) * ROWS, cols].astype(F32)
                total = total + spread[q, l, :, cols].astype(F32) * d_mix
                back = back + mm_nt((d_mix * own).astype(BF16), select[q, :, cols])
            d_values[rows, cols] = total.astype(BF16)
            d_weights[rows, :] += back
        put_value(t, mm(normed_t[...], d_values[:, cols]).astype(BF16))


def score_back(probs, d_weights, d_scores):
    total = jnp.zeros((ROWS, PAD), F32)
    for l in range(LEV):
        total = total + probs[l] * d_weights[l * ROWS : (l + 1) * ROWS, :]
    for l in range(LEV):
        rows = slice(l * ROWS, (l + 1) * ROWS)
        own = probs[l] * (d_weights[rows, :] - total) * (1.0 / math.sqrt(HEAD))
        d_scores[rows, :] = own.astype(BF16)


def token_back(px, unit, inv, w_value, wq_high, d_values, d_scores, small):
    small[48:SMALL, :] = jnp.zeros((SMALL - 48, small.shape[1]), F32)

    @pl.loop(0, LEV)
    def _(l):
        rows = pl.ds(pl.multiple_of(l * ROWS, ROWS), ROWS)
        d_normed = mm_nt(d_values[rows, :], w_value[...]) + mm(d_scores[rows, :], wq_high[...])
        own = unit[l]
        inverse = inv[l][:, :1]
        d_token = inverse * (
            d_normed
            - jnp.mean(d_normed, axis=-1, keepdims=True)
            - own * jnp.mean(d_normed * own, axis=-1, keepdims=True)
        )
        d_token = d_token.astype(BF16)
        small[48:128, :] += mm(px[l], d_token)
        small[pl.ds(128 + l, 1), :] = jnp.sum(d_token.astype(F32), axis=0, keepdims=True)


def local_kernel(
    px, w_embed, level_embed, latents, w_query, w_key, w_value, w_out, w_up, w_down, cot,
    pooled, up_all, down_all, out_all, value_all, small_all,
    select, wq_high, wq_low, level_rows, unit, inv, normed, normed_t, values, scores, weights, spread, mixed,
    attended, pool_sum, d_att, d_att_b, d_mixed, d_values, d_weights, d_scores, small,
):
    prepare(latents, w_query, w_key, select, wq_high, wq_low)
    forward(
        px, w_embed, level_embed, w_value, wq_high, wq_low, level_rows, unit, inv, normed, normed_t, values, scores
    )
    softmax(scores, weights)
    mix(weights, select, values, spread, mixed)
    attend(latents, mixed, w_out, attended)

    def put_up(t, block):
        for core in range(2):
            for z_lo in range(2):
                for y in range(4):
                    start = core * 128 + z_lo * 64 + y * 16
                    up_all[core, t // 2, y, t % 2 * 2 + z_lo] = block[start : start + 16]

    def put_down(t, block):
        for core in range(2):
            for z_lo in range(2):
                for y in range(4):
                    start = core * 128 + z_lo * 64 + y * 16
                    down_all[core, y, t % 2 * 2 + z_lo, t // 2] = block[start : start + 16]

    def put_value(t, block):
        value_all[t // 2, pl.ds(t % 2 * 2, 2)] = block.reshape(2, 4, 4, 16, TILE)

    feed_forward(attended, cot, w_up, w_down, pool_sum, d_att, put_up, put_down)
    pooled[...] = pool_sum[...].astype(BF16)
    d_att_b[...] = d_att[...].astype(BF16)
    d_mixed[...] = mm_nt(d_att_b[...], w_out[...]).astype(BF16)
    for half in range(2):
        block = mm_tn(mixed[...], d_att_b[:, half * TILE : (half + 1) * TILE]).astype(BF16)
        out_all[half] = block.reshape(4, 4, 4, 16, TILE)
    value_back(spread, d_mixed, values, normed_t, select, d_values, d_weights, put_value)
    score_back(scores, d_weights, d_scores)
    token_back(px, unit, inv, w_value, wq_high, d_values, d_scores, small)
    small[0:48, :] = mm_tn(d_scores[...], normed[...])[0:48, :]
    for q in range(LAT):
        small[136 + q : 137 + q, :] = jnp.sum(d_att[q * ROWS : (q + 1) * ROWS, :], axis=0, keepdims=True)
    small_all[...] = small[...].astype(BF16).reshape(small_all.shape)


def local_part(px, w_embed, level_embed, latents, w_query, w_key, w_value, w_out, w_up, w_down, cot):
    width, inner, ffn = w_key.shape[0], w_key.shape[1], w_up.shape[1]
    every, pairs = LEV * ROWS, LAT * ROWS
    shape = jax.ShapeDtypeStruct
    whole = pl.BlockSpec(memory_space=pltpu.VMEM)
    return pl.pallas_call(
        local_kernel,
        out_shape=(
            shape((pairs, width), BF16),
            shape((2, 4, 4, 4, 16, width), BF16),
            shape((2, 4, 4, 4, 16, width), BF16),
            shape((2, 4, 4, 4, 16, TILE), BF16),
            shape((2, 4, 4, 4, 16, TILE), BF16),
            shape((4, SMALL // 4, width), BF16),
        ),
        in_specs=[whole] * 11,
        out_specs=(whole,) * 6,
        scratch_shapes=[
            pltpu.VMEM((LAT, PAD, inner), BF16),
            pltpu.VMEM((PAD, width), BF16),
            pltpu.VMEM((PAD, width), BF16),
            pltpu.VMEM((LEV, width), F32),
            pltpu.VMEM((LEV, ROWS, width), F32),
            pltpu.VMEM((LEV, ROWS, PAD), F32),
            pltpu.VMEM((every, width), BF16),
            pltpu.VMEM((width, every), BF16),
            pltpu.VMEM((LEV, ROWS, inner), BF16),
            pltpu.VMEM((LEV, ROWS, PAD), F32),
            pltpu.VMEM((every, PAD), BF16),
            pltpu.VMEM((LAT, LEV, ROWS, inner), BF16),
            pltpu.VMEM((pairs, inner), BF16),
            pltpu.VMEM((pairs, width), BF16),
            pltpu.VMEM((pairs, width), F32),
            pltpu.VMEM((pairs, width), F32),
            pltpu.VMEM((pairs, width), BF16),
            pltpu.VMEM((pairs, inner), BF16),
            pltpu.VMEM((every, inner), BF16),
            pltpu.VMEM((every, PAD), F32),
            pltpu.VMEM((every, PAD), BF16),
            pltpu.VMEM((SMALL, width), F32),
        ],
        compiler_params=pltpu.CompilerParams(vmem_limit_bytes=60 * 1024 * 1024),
        name="local_part",
    )(px, w_embed, level_embed, latents, w_query, w_key, w_value, w_out, w_up, w_down, cot)

MESH = pl.DeviceIdType.MESH
SEMS = 112


def place():
    var, lon = lax.axis_index("var"), lax.axis_index("lon")
    return {
        "var": var,
        "lon": lon,
        "x": lon // 4,
        "y": var % 4,
        "z": (lon // 2) % 2 * 2 + var // 4,
        "core": lon % 2,
    }


SIZES = {"x": 4, "y": 4, "z": 4, "core": 2, "var": 8}


def peer(at, axis, index):
    var, lon = at["var"], at["lon"]
    if axis == "core":
        return var, lon - at["core"] + index
    if axis == "x":
        return var, index * 4 + lon % 4
    if axis == "y":
        return var - at["y"] + index, lon
    if axis == "z":
        return (index % 2) * 4 + at["y"], at["x"] * 4 + (index // 2) * 2 + at["core"]
    return index, lon


def greet(at):
    barrier = pltpu.get_barrier_semaphore()
    others = [peer(at, "var", (at["var"] + d) % 8) for d in range(1, 8)]
    others += [peer(at, "x", (at["x"] + d) % 4) for d in range(1, 4)]
    others += [peer(at, "core", 1 - at["core"])]
    far = (1 - at["z"] // 2) * 2
    others += [peer(at, "z", far), peer(at, "z", far + 1)]
    for other in others:
        pl.semaphore_signal(barrier, inc=1, device_id=other, device_id_type=MESH)
    pl.semaphore_wait(barrier, len(others))


class Wires:
    def __init__(self, at, send_sem, recv_sem):
        self.at, self.send_sem, self.recv_sem, self.used = at, send_sem, recv_sem, 0

    def copy(self, src, dst, device):
        slot = self.used
        self.used += 1
        return pltpu.make_async_remote_copy(
            src_ref=src,
            dst_ref=dst,
            send_sem=self.send_sem.at[slot],
            recv_sem=self.recv_sem.at[slot],
            device_id=device,
            device_id_type=MESH,
        )


class Scatter:
    def __init__(self, wires, axis, src, recv, out):
        self.wires, self.axis, self.src, self.recv, self.out = wires, axis, src, recv, out

    def start(self):
        at, axis, size = self.wires.at, self.axis, SIZES[self.axis]
        self.copies = []
        for d in range(1, size):
            to = (at[axis] + d) % size
            copy = self.wires.copy(self.src.at[to], self.recv.at[d - 1], peer(at, axis, to))
            copy.start()
            self.copies.append(copy)

    def finish(self):
        for copy in self.copies:
            copy.wait()
        own, count = self.wires.at[self.axis], len(self.copies)

        def add(index):
            total = self.src[(own, *index)].astype(F32)
            for d in range(count):
                total = total + self.recv[(d, *index)].astype(F32)
            self.out[index] = total.astype(BF16)

        shape = self.out.shape
        if math.prod(shape) > 65536:

            @pl.loop(0, shape[0])
            def _(i):
                add((i,) + (slice(None),) * (len(shape) - 1))

        else:
            add((slice(None),) * len(shape))


class Total:
    def __init__(self, wires, axis, src, recv, out):
        self.wires, self.axis, self.src, self.recv, self.out = wires, axis, src, recv, out

    def start(self):
        at, axis, size = self.wires.at, self.axis, SIZES[self.axis]
        self.copies = []
        for d in range(1, size):
            to = (at[axis] + d) % size
            copy = self.wires.copy(self.src, self.recv.at[d - 1], peer(at, axis, to))
            copy.start()
            self.copies.append(copy)

    def finish(self):
        for copy in self.copies:
            copy.wait()
        total = self.src[...].astype(F32)
        for d in range(len(self.copies)):
            total = total + self.recv[d].astype(F32)
        self.out[...] = total.astype(BF16)


class Gather:
    def __init__(self, wires, axis, full):
        self.wires, self.axis, self.full = wires, axis, full

    def start(self):
        at, axis, size = self.wires.at, self.axis, SIZES[self.axis]
        own = self.full.at[at[axis]]
        self.copies = []
        for d in range(1, size):
            copy = self.wires.copy(own, own, peer(at, axis, (at[axis] + d) % size))
            copy.start()
            self.copies.append(copy)

    def finish(self):
        for copy in self.copies:
            copy.wait()


class Chain:
    def __init__(self, steps):
        self.steps, self.next = steps, 0

    def advance(self):
        if self.next > 0:
            self.steps[self.next - 1].finish()
        if self.next < len(self.steps):
            self.steps[self.next].start()
        self.next += 1


def spread_chain(wires, axes, src, recvs, sums, tail, last):
    steps, block = [], src
    for axis, recv, out in zip(("core", *axes), recvs, (*sums, last)):
        steps.append(Scatter(wires, axis, block, recv, out))
        block = out
    return Chain(steps + tail)


def whole_chain(wires, axes, src, recvs, sums, full):
    at = wires.at
    where = [at["core"], *(at[axis] for axis in axes)]
    tail = [
        Gather(wires, axis, full.at[tuple(where[:depth])] if depth else full)
        for depth, axis in reversed(list(enumerate(("core", *axes))))
    ]
    return spread_chain(wires, axes, src, recvs, sums, tail, full.at[tuple(where)])


def part_chain(wires, axes, src, recvs, sums, full):
    last = full.at[wires.at["var"]]
    return spread_chain(wires, axes, src, recvs, sums, [Gather(wires, "var", full)], last)


def small_chain(wires, src, recvs, sums, full):
    own = full.at[wires.at["y"]]
    return Chain([
        Total(wires, "core", src, recvs[0], sums[0]),
        Scatter(wires, "y", sums[0], recvs[1], sums[1]),
        Total(wires, "x", sums[1], recvs[2], sums[2]),
        Total(wires, "z", sums[2], recvs[3], own),
        Gather(wires, "y", full),
    ])


def chain_scratch(width):
    block = (16, width)
    recvs = [
        pltpu.VMEM((1, 4, 4, 4, *block), BF16),
        pltpu.VMEM((3, 4, 4, *block), BF16),
        pltpu.VMEM((3, 4, *block), BF16),
        pltpu.VMEM((3, *block), BF16),
    ]
    sums = [
        pltpu.VMEM((4, 4, 4, *block), BF16),
        pltpu.VMEM((4, 4, *block), BF16),
        pltpu.VMEM((4, *block), BF16),
    ]
    return recvs, sums


def small_scratch(width):
    block = (SMALL // 4, width)
    recvs = [
        pltpu.VMEM((1, 4, *block), BF16),
        pltpu.VMEM((3, *block), BF16),
        pltpu.VMEM((3, *block), BF16),
        pltpu.VMEM((3, *block), BF16),
    ]
    sums = [pltpu.VMEM((4, *block), BF16), pltpu.VMEM(block, BF16), pltpu.VMEM(block, BF16)]
    return recvs, sums


def sums_kernel(up, down, out, value, small, up_all, down_all, out_all, value_all, small_all, scratch, send_sem, recv_sem):
    at = place()
    greet(at)
    wires = Wires(at, send_sem, recv_sem)
    chains = [
        part_chain(wires, ("y", "z", "x"), down, *scratch[0], down_all),
        part_chain(wires, ("x", "y", "z"), up, *scratch[1], up_all),
        whole_chain(wires, ("z", "x", "y"), out, *scratch[2], out_all),
        whole_chain(wires, ("z", "x", "y"), value, *scratch[3], value_all),
        small_chain(wires, small, *scratch[4], small_all),
    ]
    while any(chain.next <= len(chain.steps) for chain in chains):
        for chain in chains:
            if chain.next <= len(chain.steps):
                chain.advance()


def sums_part(up, down, out, value, small):
    width = up.shape[-1]
    shape = jax.ShapeDtypeStruct
    whole = pl.BlockSpec(memory_space=pltpu.VMEM)
    return pl.pallas_call(
        sums_kernel,
        out_shape=(
            shape((8, 16, width), BF16),
            shape((8, 16, width), BF16),
            shape(out.shape, BF16),
            shape(value.shape, BF16),
            shape(small.shape, BF16),
        ),
        in_specs=[whole] * 5,
        out_specs=(whole,) * 5,
        scratch_shapes=[
            [chain_scratch(width), chain_scratch(width), chain_scratch(TILE), chain_scratch(TILE), small_scratch(width)],
            pltpu.SemaphoreType.DMA((SEMS,)),
            pltpu.SemaphoreType.DMA((SEMS,)),
        ],
        compiler_params=pltpu.CompilerParams(
            vmem_limit_bytes=60 * 1024 * 1024, collective_id=0, has_side_effects=True
        ),
        name="sums_part",
    )(up, down, out, value, small)


def finish_kernel(
    small, value_all, out_all, up_part, down_part, latents, w_query, w_key,
    grad_embed, grad_level, grad_lat, grad_query, grad_key, grad_value, grad_out, grad_up, grad_down,
):
    grad_up[...] = up_part[...].reshape(ROWS, -1).astype(F32).T
    grad_down[...] = down_part[...].reshape(ROWS, -1).astype(F32)
    rest = small[...].reshape(SMALL, -1)
    grad_embed[...] = rest[48:128, :].astype(F32)
    grad_level[...] = rest[128:136, :].astype(F32)
    width, inner = w_key.shape
    for t in range(4):
        block = value_all[t // 2, t % 2 * 2 : t % 2 * 2 + 2].reshape(width, TILE)
        grad_value[:, t * TILE : (t + 1) * TILE] = block.astype(F32)
    for half in range(2):
        grad_out[:, half * TILE : (half + 1) * TILE] = out_all[half].reshape(inner, TILE).astype(F32)
    rows = query_rows(latents[...], w_query[...])
    total = rest[0:48, :]
    grad_key[...] = mm_tn(total, rows[0:48, :])
    spread = mm(total, w_key[...])
    row = lax.broadcasted_iota(jnp.int32, (48, inner), 0)
    head = lax.broadcasted_iota(jnp.int32, (48, inner), 1) // HEAD
    own = []
    for q in range(LAT):
        own.append(jnp.sum(jnp.where(row == q * HEADS + head, spread, 0.0), axis=0, keepdims=True))
    d_queries = jnp.concatenate(own, axis=0)
    high, low = split(d_queries)
    grad_query[...] = mm_tn(latents[...], high) + mm_tn(latents[...], low)
    grad_lat[...] = rest[136:139, :].astype(F32) + mm_nt(high, w_query[...]) + mm_nt(low, w_query[...])


def finish(small, value_all, out_all, up_part, down_part, latents, w_query, w_key):
    width, inner = w_key.shape
    shape = jax.ShapeDtypeStruct
    whole = pl.BlockSpec(memory_space=pltpu.VMEM)
    return pl.pallas_call(
        finish_kernel,
        out_shape=(
            shape((80, width), F32),
            shape((LEV, width), F32),
            shape((LAT, width), F32),
            shape((width, inner), F32),
            shape((width, inner), F32),
            shape((width, inner), F32),
            shape((inner, width), F32),
            shape((width, ROWS), F32),
            shape((ROWS, width), F32),
        ),
        in_specs=[whole] * 8,
        out_specs=(whole,) * 9,
        compiler_params=pltpu.CompilerParams(vmem_limit_bytes=60 * 1024 * 1024),
        name="finish",
    )(small, value_all, out_all, up_part, down_part, latents, w_query, w_key)


def on_device(
    pixels, w_embed, level_embed, latents, w_query, w_key, w_value, w_out, w_up, w_down, cotangent
):
    width = w_embed.shape[1]
    own = pixels.reshape(80, LEV, ROWS)
    px = lax.all_to_all(own, "var", split_axis=1, concat_axis=1, tiled=True)
    px = jnp.transpose(px, (1, 0, 2))
    pooled, up_all, down_all, out_all, value_all, small = local_part(
        px, w_embed, level_embed, latents, w_query, w_key, w_value, w_out, w_up, w_down,
        cotangent.reshape(LAT * ROWS, width),
    )
    up_part, down_part, out_all, value_all, small = sums_part(up_all, down_all, out_all, value_all, small)
    grads = finish(small, value_all, out_all, up_part, down_part, latents, w_query, w_key)
    return (pooled.reshape(LAT, ROWS, width), *grads)


def solution(mesh):
    return jax.shard_map(
        on_device,
        mesh=mesh,
        in_specs=(
            P("var", None, None, "lon"),
            *([P()] * 9),
            P(None, ("lon", "var"), None),
        ),
        out_specs=(
            P(None, ("lon", "var"), None),
            *([P()] * 7),
            P(None, "lon"),
            P("lon", None),
        ),
        check_vma=False,
    )
```

```python
import functools
import math

import jax
import jax.numpy as jnp
from jax import lax
from jax.experimental import pallas as pl
from jax.experimental.pallas import tpu as pltpu
from jax.sharding import PartitionSpec as P

F32 = jnp.float32
BF16 = jnp.bfloat16
EPSILON = 1e-05
HEADS = 16
HEAD = 64
LEV = 8
LAT = 3
ROWS = 128
TILE = 256
PAD = 128
GELU_C = math.sqrt(2.0 / math.pi)
GELU_A = 0.044715


def mm(left, right):
    return lax.dot_general(left, right, (((1,), (0,)), ((), ())), preferred_element_type=F32)


def mm_nt(left, right):
    return lax.dot_general(left, right, (((1,), (1,)), ((), ())), preferred_element_type=F32)


def mm_tn(left, right):
    return lax.dot_general(left, right, (((0,), (0,)), ((), ())), preferred_element_type=F32)


def split(value):
    high = value.astype(BF16)
    return high, (value - high.astype(F32)).astype(BF16)


def head_rows(inner):
    row = lax.broadcasted_iota(jnp.int32, (PAD, inner), 0)
    head = lax.broadcasted_iota(jnp.int32, (PAD, inner), 1) // HEAD
    return row, head


def query_rows(latents, w_query):
    queries = mm(latents, w_query).astype(BF16).astype(F32)
    inner = queries.shape[1]
    row, head = head_rows(inner)
    spread = jnp.zeros((PAD, inner), F32)
    for q in range(LAT):
        spread = jnp.where(row == q * HEADS + head, queries[q : q + 1, :], spread)
    return spread.astype(BF16)


def prepare(latents, w_query, w_key, select, wq_high, wq_low):
    inner = w_key.shape[1]
    row, head = head_rows(inner)
    for q in range(LAT):
        select[q] = jnp.where(row == q * HEADS + head, 1.0, 0.0).astype(BF16)
    folded = mm_nt(query_rows(latents[...], w_query[...]), w_key[...])
    high, low = split(folded)
    wq_high[...] = high
    wq_low[...] = low


def forward(
    px, w_embed, level_embed, w_value, wq_high, wq_low, level_rows, unit, inv, normed, normed_t, values, scores
):
    level_rows[...] = level_embed[...].astype(F32)

    @pl.loop(0, LEV)
    def _(l):
        token = mm_tn(px[l].reshape(80, ROWS), w_embed[...]) + level_rows[pl.ds(l, 1), :]
        token = token.astype(BF16).astype(F32)
        center = token - jnp.mean(token, axis=-1, keepdims=True)
        inverse = lax.rsqrt(jnp.mean(center * center, axis=-1, keepdims=True) + EPSILON)
        own = center * inverse
        unit[l] = own
        inv[l] = jnp.broadcast_to(inverse, (ROWS, PAD))
        own = own.astype(BF16)
        normed[pl.ds(pl.multiple_of(l * ROWS, ROWS), ROWS), :] = own
        scores[l] = (mm_nt(own, wq_high[...]) + mm_nt(own, wq_low[...])) * (1.0 / math.sqrt(HEAD))
        values[l] = mm(own, w_value[...]).astype(BF16)

    normed_t[...] = normed[...].T


def softmax(scores, weights):
    highest = scores[0]
    for l in range(1, LEV):
        highest = jnp.maximum(highest, scores[l])
    total = jnp.zeros_like(highest)
    for l in range(LEV):
        expo = jnp.exp(scores[l] - highest)
        scores[l] = expo
        total = total + expo
    for l in range(LEV):
        prob = scores[l] / total
        scores[l] = prob
        weights[l * ROWS : (l + 1) * ROWS, :] = prob.astype(BF16)


def mix(weights, select, values, spread, mixed):
    inner = values.shape[2]

    @pl.loop(0, inner // TILE)
    def _(t):
        cols = pl.ds(pl.multiple_of(t * TILE, TILE), TILE)
        for q in range(LAT):
            total = jnp.zeros((ROWS, TILE), F32)
            for l in range(LEV):
                own = mm(weights[l * ROWS : (l + 1) * ROWS, :], select[q, :, cols])
                spread[q, l, :, cols] = own.astype(BF16)
                total = total + own * values[l, :, cols].astype(F32)
            mixed[q * ROWS : (q + 1) * ROWS, cols] = total.astype(BF16)


def attend(latents, mixed, w_out, attended):
    for q in range(LAT):
        rows = slice(q * ROWS, (q + 1) * ROWS)
        own = mm(mixed[rows, :], w_out[...]) + latents[q : q + 1, :].astype(F32)
        attended[rows, :] = own.astype(BF16)


def feed_forward(attended, cot, w_up, w_down, pool_sum, d_att, hidden, d_pre):
    pool_sum[...] = attended[...].astype(F32)
    d_att[...] = cot[...].astype(F32)

    @pl.loop(0, w_up.shape[1] // TILE)
    def _(t):
        cols = pl.ds(pl.multiple_of(t * TILE, TILE), TILE)
        pre = mm(attended[...], w_up[:, cols])
        square = pre * pre
        bent = jnp.tanh(GELU_C * (pre + GELU_A * (square * pre)))
        half = 0.5 * (1.0 + bent)
        own = (pre * half).astype(BF16)
        slope = half + 0.5 * pre * (1.0 - bent * bent) * (GELU_C * (1.0 + 3.0 * GELU_A * square))
        back = (mm_nt(cot[...], w_down[cols, :]) * slope).astype(BF16)
        hidden[:, cols] = own
        d_pre[:, cols] = back
        pool_sum[...] += mm(own, w_down[cols, :])
        d_att[...] += mm_nt(back, w_up[:, cols])


def value_grad(t, spread, d_mixed, normed_t, d_values):
    cols = slice(t * TILE, (t + 1) * TILE)
    for l in range(LEV):
        total = jnp.zeros((ROWS, TILE), F32)
        for q in range(LAT):
            d_mix = d_mixed[q * ROWS : (q + 1) * ROWS, cols].astype(F32)
            total = total + spread[q, l, :, cols].astype(F32) * d_mix
        d_values[l * ROWS : (l + 1) * ROWS, cols] = total.astype(BF16)
    return mm(normed_t[...], d_values[:, cols]).astype(BF16)


def weight_grad(d_mixed, values, select, d_weights):
    d_weights[...] = jnp.zeros_like(d_weights)

    @pl.loop(0, values.shape[2] // TILE)
    def _(t):
        cols = pl.ds(pl.multiple_of(t * TILE, TILE), TILE)
        for l in range(LEV):
            own = values[l, :, cols].astype(F32)
            back = jnp.zeros((ROWS, PAD), F32)
            for q in range(LAT):
                d_mix = d_mixed[q * ROWS : (q + 1) * ROWS, cols].astype(F32)
                back = back + mm_nt((d_mix * own).astype(BF16), select[q, :, cols])
            d_weights[l * ROWS : (l + 1) * ROWS, :] += back


def score_back(probs, d_weights, d_scores):
    total = jnp.zeros((ROWS, PAD), F32)
    for l in range(LEV):
        total = total + probs[l] * d_weights[l * ROWS : (l + 1) * ROWS, :]
    for l in range(LEV):
        rows = slice(l * ROWS, (l + 1) * ROWS)
        own = probs[l] * (d_weights[rows, :] - total) * (1.0 / math.sqrt(HEAD))
        d_scores[rows, :] = own.astype(BF16)


def token_back(levels, px, unit, inv, w_value, wq_high, d_values, d_scores, small, rest):
    for l in levels:
        rows = slice(l * ROWS, (l + 1) * ROWS)
        d_normed = mm_nt(d_values[rows, :], w_value[...]) + mm(d_scores[rows, :], wq_high[...])
        own = unit[l]
        inverse = inv[l][:, :1]
        d_token = inverse * (
            d_normed
            - jnp.mean(d_normed, axis=-1, keepdims=True)
            - own * jnp.mean(d_normed * own, axis=-1, keepdims=True)
        )
        d_token = d_token.astype(BF16)
        small[48:128, :] += mm(px[l].reshape(80, ROWS), d_token)
        rest[l : l + 1, :] = jnp.sum(d_token.astype(F32), axis=0, keepdims=True)


MESH = pl.DeviceIdType.MESH
SEMS = 176


def locate(var, lon):
    return {
        "var": var,
        "lon": lon,
        "x": lon // 4,
        "y": var % 4,
        "z": (lon // 2) % 2 * 2 + var // 4,
        "core": lon % 2,
    }


def place():
    return locate(lax.axis_index("var"), lax.axis_index("lon"))


SIZES = {"x": 4, "y": 4, "z": 4, "core": 2, "var": 8}


def peer(at, axis, index):
    var, lon = at["var"], at["lon"]
    if axis == "core":
        return var, lon - at["core"] + index
    if axis == "x":
        return var, index * 4 + lon % 4
    if axis == "y":
        return var - at["y"] + index, lon
    if axis == "z":
        return (index % 2) * 4 + at["y"], at["x"] * 4 + (index // 2) * 2 + at["core"]
    return index, lon


def greet(at):
    barrier = pltpu.get_barrier_semaphore()
    others = [peer(at, "core", 1 - at["core"])]
    steps = range(4)
    for i, j in [(i, j) for i in steps for j in steps if i or j]:
        along = locate(*peer(at, "y", (at["y"] + i) % 4))
        others.append(peer(along, "x", (at["x"] + j) % 4))
        if j:
            others.append(peer(along, "z", (at["z"] + j) % 4))
    for other in others:
        pl.semaphore_signal(barrier, inc=1, device_id=other, device_id_type=MESH)
    pl.semaphore_wait(barrier, len(others))


class Wires:
    def __init__(self, at, send_sem, recv_sem):
        self.at, self.send_sem, self.recv_sem, self.used = at, send_sem, recv_sem, 0

    def copy(self, src, dst, device):
        slot = self.used
        self.used += 1
        return pltpu.make_async_remote_copy(
            src_ref=src,
            dst_ref=dst,
            send_sem=self.send_sem.at[slot],
            recv_sem=self.recv_sem.at[slot],
            device_id=device,
            device_id_type=MESH,
        )


HOP = 2.7
LINK = 46e3
CHIP = 700e3


def size_of(ref):
    return 2 * math.prod(ref.shape)


def add_into(out, where, parts):
    total = parts[0][...].astype(F32)
    for part in parts[1:]:
        total = total + part[...].astype(F32)
    out[where] = total.astype(BF16)


class Step:
    def __init__(self, wires, axis):
        self.wires, self.axis, self.copies = wires, axis, []

    def send(self, src, dst, index):
        copy = self.wires.copy(src, dst, peer(self.wires.at, self.axis, index))
        copy.start()
        self.copies.append(copy)

    def others(self):
        own, size = self.wires.at[self.axis], SIZES[self.axis]
        return [(own + d) % size for d in range(1, size)]

    def cost(self, block):
        if self.axis == "core":
            return HOP / 2 + block / CHIP
        return HOP + block * {"x": 2, "y": 2, "z": 2, "var": 4}[self.axis] / LINK

    def wait(self):
        for copy in self.copies:
            copy.wait()


class Scatter(Step):
    def __init__(self, wires, axis, src, recv, out):
        super().__init__(wires, axis)
        self.src, self.recv, self.out = src, recv, out
        self.time = self.cost(size_of(out))

    def start(self):
        for d, to in enumerate(self.others()):
            self.send(self.src.at[to], self.recv.at[d], to)

    def finish(self):
        self.wait()
        own, count = self.wires.at[self.axis], len(self.copies)
        shape = self.out.shape

        def add(*index):
            refs = [self.src.at[own]] + [self.recv.at[d] for d in range(count)]
            where = index if index else (slice(None),) * len(shape)
            add_into(self.out, where, [ref.at[where] for ref in refs])

        if math.prod(shape) > 65536:

            @pl.loop(0, shape[0])
            def _(i):
                add(i, *((slice(None),) * (len(shape) - 1)))

        else:
            add()


class Total(Step):
    def __init__(self, wires, axis, src, recv, out):
        super().__init__(wires, axis)
        self.src, self.recv, self.out = src, recv, out
        self.time = self.cost(size_of(src))

    def start(self):
        for d, to in enumerate(self.others()):
            self.send(self.src, self.recv.at[d], to)

    def finish(self):
        self.wait()
        add_into(self.out, ..., [self.src] + [self.recv.at[d] for d in range(len(self.copies))])


class Gather(Step):
    def __init__(self, wires, axis, full):
        super().__init__(wires, axis)
        self.full = full
        self.time = self.cost(size_of(full) // full.shape[0])

    def start(self):
        own = self.full.at[self.wires.at[self.axis]]
        for to in self.others():
            self.send(own, own, to)

    def finish(self):
        self.wait()


class Plane(Step):
    def __init__(self, wires, axes):
        super().__init__(wires, axes)
        self.hop = HOP + 1.0

    def here(self):
        return tuple(self.wires.at[axis] for axis in self.axis)

    def others(self):
        first, second = self.here()
        ring = [(i, j) for i in range(4) for j in range(4) if i or j]
        return [((first + i) % 4, (second + j) % 4) for i, j in ring]

    def send(self, src, dst, index):
        at = dict(self.wires.at)
        for axis, place in zip(self.axis, index):
            var, lon = peer(at, axis, place)
            at = locate(var, lon)
        copy = self.wires.copy(src, dst, (var, lon))
        copy.start()
        self.copies.append(copy)


class PlaneScatter(Plane):
    def __init__(self, wires, axes, src, recv, out):
        super().__init__(wires, axes)
        self.src, self.recv, self.out = src, recv, out
        self.time = self.hop + size_of(out) * 8 / LINK

    def start(self):
        for d, to in enumerate(self.others()):
            self.send(self.src.at[to], self.recv.at[d], to)

    def finish(self):
        self.wait()
        parts = [self.src.at[self.here()]] + [self.recv.at[d] for d in range(15)]
        if len(self.out.shape) == 2:
            add_into(self.out, ..., parts)
        else:
            for k in range(self.out.shape[0]):
                add_into(self.out, (k,), [part.at[k] for part in parts])


class PlaneGather(Plane):
    def __init__(self, wires, axes, full):
        super().__init__(wires, axes)
        self.full = full
        self.time = self.hop + size_of(full) / 16 * 8 / LINK

    def start(self):
        own = self.full.at[self.here()]
        for to in self.others():
            self.send(own, own, to)

    def finish(self):
        self.wait()


def ring(at, axis):
    own = at[axis]
    return own, own + 1 - 2 * (own % 2), 3 - own, (own + 2) % 4


HALVES = (slice(0, 2), slice(2, 4))


class FoldFirst(Step):
    def __init__(self, wires, axis, src, recv, out):
        super().__init__(wires, axis)
        self.src, self.recv, self.out = src, recv, out
        self.time = HOP + size_of(out) / 2 / LINK

    def start(self):
        own, near, back, far = ring(self.wires.at, self.axis)
        for half, to in ((0, back), (1, near)):
            for slot, block in ((1, far), (0, to)):
                self.send(self.src.at[block, HALVES[half]], self.recv.at[half, slot], to)

    def finish(self):
        self.wait()
        own, near, back, far = ring(self.wires.at, self.axis)
        for half, other in ((0, near), (1, back)):
            for slot, block in ((1, other), (0, own)):
                for k in range(2):
                    add_into(
                        self.out,
                        (half, slot, k),
                        [self.src.at[block, 2 * half + k], self.recv.at[half, slot, k]],
                    )


class FoldSecond(Step):
    def __init__(self, wires, axis, src, recv, out):
        super().__init__(wires, axis)
        self.src, self.recv, self.out = src, recv, out
        self.time = HOP + size_of(out) / 2 / LINK

    def start(self):
        own, near, back, far = ring(self.wires.at, self.axis)
        for half, to in ((0, near), (1, back)):
            self.send(self.src.at[half, 1], self.recv.at[half], to)

    def finish(self):
        self.wait()
        for half in range(2):
            add_into(self.out, (HALVES[half],), [self.src.at[half, 0], self.recv.at[half]])


class Chain:
    def __init__(self, steps):
        self.steps, self.next = steps, 0

    def advance(self):
        if self.next > 0:
            self.steps[self.next - 1].finish()
        if self.next < len(self.steps):
            self.steps[self.next].start()
        self.next += 1


class Clock:
    def __init__(self):
        self.now, self.active = 0.0, []

    def begin(self, chain):
        chain.advance()
        chain.due = self.now + chain.steps[0].time
        self.active.append(chain)

    def step(self, chain):
        chain.advance()
        if chain.next > len(chain.steps):
            self.active.remove(chain)
        else:
            chain.due = max(self.now, chain.due) + chain.steps[chain.next - 1].time

    def passed(self, time):
        self.now += time
        for chain in sorted(self.active, key=lambda chain: chain.due):
            if chain.due <= self.now:
                self.step(chain)

    def drain(self):
        while self.active:
            chain = min(self.active, key=lambda chain: chain.due)
            self.now = max(self.now, chain.due)
            self.step(chain)


def spread_steps(wires, axes, src, recvs, sums, last):
    first, second, third = axes
    return [
        Scatter(wires, "core", src, recvs[0], sums[0]),
        FoldFirst(wires, first, sums[0], recvs[1], sums[1]),
        FoldSecond(wires, first, sums[1], recvs[2], sums[2]),
        Scatter(wires, second, sums[2], recvs[3], sums[3]),
        Scatter(wires, third, sums[3], recvs[4], last),
    ]


def whole_chain(wires, axes, src, recvs, sums, full):
    at = wires.at
    core, first, second, third = at["core"], *(at[axis] for axis in axes)
    return Chain([
        Scatter(wires, "core", src, recvs[0], sums[0]),
        PlaneScatter(wires, axes[:2], sums[0], recvs[1], sums[1]),
        Scatter(wires, axes[2], sums[1], recvs[2], full.at[core, first, second, third]),
        Gather(wires, axes[2], full.at[core, first, second]),
        PlaneGather(wires, axes[:2], full.at[core]),
        Gather(wires, "core", full),
    ])


def part_chain(wires, axes, src, recvs, sums, full):
    steps = spread_steps(wires, axes, src, recvs, sums, full.at[wires.at["var"]])
    return Chain(steps + [Gather(wires, "var", full)])


def small_chain(wires, src, recvs, sums, full):
    core, x, y = wires.at["core"], wires.at["x"], wires.at["y"]
    return Chain([
        Scatter(wires, "core", src, recvs[0], sums[0]),
        PlaneScatter(wires, ("x", "y"), sums[0], recvs[1], sums[1]),
        Total(wires, "z", sums[1], recvs[2], full.at[core, x, y]),
        PlaneGather(wires, ("x", "y"), full.at[core]),
        Gather(wires, "core", full),
    ])


def chain_scratch(width):
    block = (16, width)
    recvs = [
        pltpu.VMEM((1, 4, 4, 4, *block), BF16),
        pltpu.VMEM((2, 2, 2, 4, *block), BF16),
        pltpu.VMEM((2, 2, 4, *block), BF16),
        pltpu.VMEM((3, 4, *block), BF16),
        pltpu.VMEM((3, *block), BF16),
    ]
    sums = [
        pltpu.VMEM((4, 4, 4, *block), BF16),
        pltpu.VMEM((2, 2, 2, 4, *block), BF16),
        pltpu.VMEM((4, 4, *block), BF16),
        pltpu.VMEM((4, *block), BF16),
    ]
    return recvs, sums


def whole_scratch(width):
    block = (16, width)
    recvs = [
        pltpu.VMEM((1, 4, 4, 4, *block), BF16),
        pltpu.VMEM((15, 4, *block), BF16),
        pltpu.VMEM((3, *block), BF16),
    ]
    sums = [pltpu.VMEM((4, 4, 4, *block), BF16), pltpu.VMEM((4, *block), BF16)]
    return recvs, sums


SMALL_SHAPE = (2, 4, 4, 16, TILE)


def small_scratch():
    block = SMALL_SHAPE[3:]
    recvs = [
        pltpu.VMEM((1, 4, 4, *block), BF16),
        pltpu.VMEM((15, *block), BF16),
        pltpu.VMEM((3, *block), BF16),
    ]
    sums = [pltpu.VMEM((4, 4, *block), BF16), pltpu.VMEM(block, BF16)]
    return recvs, sums


def chain_shapes(width):
    return (2, 4, 4, 4, 16, width)


WEIGHTS = 10


def main_kernel(
    pixels, w_embed_h, level_embed_h, latents_h, w_query_h, w_key_h, w_value_h, w_out_h, w_up_h, w_down_h, cot_h,
    pooled, up_all, down_all, out_all, value_all, small_all,
    loaded, work, grads, scratch, load_sem, send_sem, recv_sem,
):
    w_embed, level_embed, latents, w_query, w_key, w_value, w_out, w_up, w_down, cot, px = loaded
    (
        select, wq_high, wq_low, level_rows, unit, inv, normed, normed_t, values, scores, weights, spread, mixed,
        attended, pool_sum, d_att, d_att_b, d_mixed, d_values, d_weights, d_scores, hidden, d_pre, small, rest,
    ) = work
    up, down, out, value, small_b = grads
    at = place()
    wires = Wires(at, send_sem, recv_sem)

    pairs = [
        (latents_h, latents), (w_query_h, w_query), (w_key_h, w_key), (w_embed_h, w_embed),
        (level_embed_h, level_embed), (w_value_h, w_value), (w_out_h, w_out), (cot_h, cot),
        (w_up_h, w_up), (w_down_h, w_down),
    ]
    loads = [pltpu.make_async_copy(src, dst, load_sem.at[i]) for i, (src, dst) in enumerate(pairs)]
    for load in loads:
        load.start()

    def patches(index):
        return pixels.at[:, :, pl.ds(pl.multiple_of(index * ROWS, ROWS), ROWS)]

    keep = pltpu.make_async_copy(patches(at["var"]), px.at[at["var"]], load_sem.at[WEIGHTS])
    keep.start()
    greet(at)
    moves = []
    for d in range(1, 8):
        to = (at["var"] + d) % 8
        move = wires.copy(patches(to), px.at[at["var"]], peer(at, "var", to))
        move.start()
        moves.append(move)

    for load in loads[:3]:
        load.wait()
    prepare(latents, w_query, w_key, select, wq_high, wq_low)
    for load in loads[3:6]:
        load.wait()
    keep.wait()
    for move in moves:
        move.wait()
    forward(
        px, w_embed, level_embed, w_value, wq_high, wq_low, level_rows, unit, inv, normed, normed_t, values, scores
    )
    softmax(scores, weights)
    mix(weights, select, values, spread, mixed)
    for load in loads[6:]:
        load.wait()
    attend(latents, mixed, w_out, attended)

    chain_down = part_chain(wires, ("z", "x", "y"), down, *scratch[0], down_all)
    chain_up = part_chain(wires, ("x", "z", "y"), up, *scratch[1], up_all)
    chain_out = whole_chain(wires, ("x", "y", "z"), out, *scratch[2], out_all)
    chain_value = whole_chain(wires, ("y", "z", "x"), value, *scratch[3], value_all)
    chain_small = small_chain(wires, small_b, *scratch[4], small_all)
    clock = Clock()

    feed_forward(attended, cot, w_up, w_down, pool_sum, d_att, hidden, d_pre)
    d_att_b[...] = d_att[...].astype(BF16)
    for half in range(2):
        block = mm_tn(mixed[...], d_att_b[:, half * TILE : (half + 1) * TILE]).astype(BF16)
        out[half] = block.reshape(4, 4, 4, 16, TILE)
    clock.begin(chain_out)
    d_mixed[...] = mm_nt(d_att_b[...], w_out[...]).astype(BF16)
    clock.passed(0.8)
    for t in range(4):
        block = value_grad(t, spread, d_mixed, normed_t, d_values)
        value[t // 2, t % 2 * 2 : t % 2 * 2 + 2] = block.reshape(2, 4, 4, 16, TILE)
        clock.passed(0.7)
    clock.begin(chain_value)

    for t in range(8):
        cols = slice(t * TILE, (t + 1) * TILE)
        block = mm_tn(hidden[:, cols], cot[...]).astype(BF16)
        for core in range(2):
            for var in range(8):
                start = core * 128 + var * 16
                down[core, t % 2 * 2 + var // 4, t // 2, var % 4] = block[start : start + 16]
        clock.passed(0.25)
    clock.begin(chain_down)
    for t in range(8):
        cols = slice(t * TILE, (t + 1) * TILE)
        block = mm_tn(d_pre[:, cols], attended[...]).astype(BF16)
        for core in range(2):
            for var in range(8):
                start = core * 128 + var * 16
                up[core, t // 2, t % 2 * 2 + var // 4, var % 4] = block[start : start + 16]
        clock.passed(0.25)
    clock.begin(chain_up)

    weight_grad(d_mixed, values, select, d_weights)
    clock.passed(2.5)
    score_back(scores, d_weights, d_scores)
    pooled[...] = pool_sum[...].astype(BF16)
    clock.passed(0.5)
    small[...] = jnp.zeros_like(small)
    rest[...] = jnp.zeros_like(rest)
    for l in range(0, LEV, 2):
        token_back((l, l + 1), px, unit, inv, w_value, wq_high, d_values, d_scores, small, rest)
        clock.passed(1.7)
    small[0:48, :] = mm_tn(d_scores[...], normed[...])[0:48, :]
    for q in range(LAT):
        rest[8 + q : 9 + q, :] = jnp.sum(d_att[q * ROWS : (q + 1) * ROWS, :], axis=0, keepdims=True)
    small_b[...] = jnp.zeros_like(small_b)
    for k in range(2):
        cols = slice(k * TILE, (k + 1) * TILE)
        small_b[0, 2 * k : 2 * k + 2] = small[:, cols].astype(BF16).reshape(2, 4, 16, TILE)
        small_b[1, 0, k] = rest[:, cols].astype(BF16)
    clock.passed(0.5)
    clock.begin(chain_small)
    clock.drain()


def main_part(pixels, w_embed, level_embed, latents, w_query, w_key, w_value, w_out, w_up, w_down, cot):
    width, inner = w_key.shape
    every, pairs = LEV * ROWS, LAT * ROWS
    shape = jax.ShapeDtypeStruct
    whole = pl.BlockSpec(memory_space=pltpu.VMEM)
    vmem = pltpu.VMEM
    arrays = (w_embed, level_embed, latents, w_query, w_key, w_value, w_out, w_up, w_down, cot)
    loaded = [vmem(array.shape, BF16) for array in arrays] + [vmem((LEV, 5, 16, ROWS), BF16)]
    work = [
        vmem((LAT, PAD, inner), BF16),
        vmem((PAD, width), BF16),
        vmem((PAD, width), BF16),
        vmem((LEV, width), F32),
        vmem((LEV, ROWS, width), F32),
        vmem((LEV, ROWS, PAD), F32),
        vmem((every, width), BF16),
        vmem((width, every), BF16),
        vmem((LEV, ROWS, inner), BF16),
        vmem((LEV, ROWS, PAD), F32),
        vmem((every, PAD), BF16),
        vmem((LAT, LEV, ROWS, inner), BF16),
        vmem((pairs, inner), BF16),
        vmem((pairs, width), BF16),
        vmem((pairs, width), F32),
        vmem((pairs, width), F32),
        vmem((pairs, width), BF16),
        vmem((pairs, inner), BF16),
        vmem((every, inner), BF16),
        vmem((every, PAD), F32),
        vmem((every, PAD), BF16),
        vmem((pairs, w_up.shape[1]), BF16),
        vmem((pairs, w_up.shape[1]), BF16),
        vmem((128, width), F32),
        vmem((16, width), F32),
    ]
    grads = [
        vmem(chain_shapes(width), BF16),
        vmem(chain_shapes(width), BF16),
        vmem(chain_shapes(TILE), BF16),
        vmem(chain_shapes(TILE), BF16),
        vmem(SMALL_SHAPE, BF16),
    ]
    return pl.pallas_call(
        main_kernel,
        out_shape=(
            shape((pairs, width), BF16),
            shape((8, 16, width), BF16),
            shape((8, 16, width), BF16),
            shape(chain_shapes(TILE), BF16),
            shape(chain_shapes(TILE), BF16),
            shape(SMALL_SHAPE, BF16),
        ),
        in_specs=[pl.BlockSpec(memory_space=pl.ANY)] * 11,
        out_specs=(whole,) * 6,
        scratch_shapes=[
            loaded,
            work,
            grads,
            [chain_scratch(width), chain_scratch(width), whole_scratch(TILE), whole_scratch(TILE), small_scratch()],
            pltpu.SemaphoreType.DMA((WEIGHTS + 1,)),
            pltpu.SemaphoreType.DMA((SEMS,)),
            pltpu.SemaphoreType.DMA((SEMS,)),
        ],
        compiler_params=pltpu.CompilerParams(
            vmem_limit_bytes=60 * 1024 * 1024, collective_id=0, has_side_effects=True
        ),
        name="main_part",
    )(pixels, w_embed, level_embed, latents, w_query, w_key, w_value, w_out, w_up, w_down, cot)


def finish_kernel(
    small_h, value_h, out_h, up_h, down_h, latents, w_query_h, w_key_h,
    grad_embed, grad_level, grad_lat, grad_up, grad_down, query_h, key_h, value_g, out_g,
    small, value_all, out_all, w_query, w_key, grad_query, grad_key, grad_value, grad_out, up_part, down_part,
    load_sem, save_sem,
):
    pairs = [
        (value_h, value_all), (out_h, out_all), (small_h, small), (w_query_h, w_query), (w_key_h, w_key),
        (up_h, up_part), (down_h, down_part),
    ]
    loads = [pltpu.make_async_copy(src, dst, load_sem.at[i]) for i, (src, dst) in enumerate(pairs)]
    for load in loads:
        load.start()
    saves = []

    def save(src, dst):
        copy = pltpu.make_async_copy(src, dst, save_sem.at[len(saves)])
        copy.start()
        saves.append(copy)

    width, inner = w_key.shape
    loads[0].wait()
    for t in range(4):
        block = value_all[t // 2, t % 2 * 2 : t % 2 * 2 + 2].reshape(width, TILE)
        cols = slice(t * TILE, (t + 1) * TILE)
        grad_value[:, cols] = block.astype(F32)
        save(grad_value.at[:, cols], value_g.at[:, cols])
    loads[1].wait()
    for half in range(2):
        cols = slice(half * TILE, (half + 1) * TILE)
        grad_out[:, cols] = out_all[half].reshape(inner, TILE).astype(F32)
        save(grad_out.at[:, cols], out_g.at[:, cols])
    for load in loads[2:5]:
        load.wait()
    sums = jnp.concatenate([small[0, 2 * k : 2 * k + 2].reshape(128, TILE) for k in range(2)], axis=1)
    rest = jnp.concatenate([small[1, 0, k] for k in range(2)], axis=1)
    total = sums[0:48, :]
    rows = query_rows(latents[...], w_query[...])
    for t in range(2):
        cols = slice(t * 512, (t + 1) * 512)
        grad_key[:, cols] = mm_tn(total, rows[0:48, cols])
        save(grad_key.at[:, cols], key_h.at[:, cols])
    spread = mm(total, w_key[...])
    row = lax.broadcasted_iota(jnp.int32, (48, inner), 0)
    head = lax.broadcasted_iota(jnp.int32, (48, inner), 1) // HEAD
    own = []
    for q in range(LAT):
        own.append(jnp.sum(jnp.where(row == q * HEADS + head, spread, 0.0), axis=0, keepdims=True))
    d_queries = jnp.concatenate(own, axis=0)
    high, low = split(d_queries)
    for t in range(2):
        cols = slice(t * 512, (t + 1) * 512)
        grad_query[:, cols] = mm_tn(latents[...], high[:, cols]) + mm_tn(latents[...], low[:, cols])
        save(grad_query.at[:, cols], query_h.at[:, cols])
    grad_lat[...] = rest[8:11, :].astype(F32) + mm_nt(high, w_query[...]) + mm_nt(low, w_query[...])
    grad_embed[...] = sums[48:128, :].astype(F32)
    grad_level[...] = rest[0:8, :].astype(F32)
    for load in loads[5:]:
        load.wait()
    grad_up[...] = up_part[...].reshape(ROWS, -1).astype(F32).T
    grad_down[...] = down_part[...].reshape(ROWS, -1).astype(F32)
    for copy in saves:
        copy.wait()


def finish(small, value_all, out_all, up_part, down_part, latents, w_query, w_key):
    width, inner = w_key.shape
    shape = jax.ShapeDtypeStruct
    whole = pl.BlockSpec(memory_space=pltpu.VMEM)
    anywhere = pl.BlockSpec(memory_space=pl.ANY)
    vmem = pltpu.VMEM
    embed, level, lat, up, down, query, key, value, out = pl.pallas_call(
        finish_kernel,
        out_shape=(
            shape((80, width), F32),
            shape((LEV, width), F32),
            shape((LAT, width), F32),
            shape((width, ROWS), F32),
            shape((ROWS, width), F32),
            shape((width, inner), F32),
            shape((width, inner), F32),
            shape((width, inner), F32),
            shape((inner, width), F32),
        ),
        in_specs=[anywhere] * 5 + [whole] + [anywhere] * 2,
        out_specs=(whole,) * 5 + (anywhere,) * 4,
        scratch_shapes=[
            vmem(small.shape, BF16),
            vmem(value_all.shape, BF16),
            vmem(out_all.shape, BF16),
            vmem(w_query.shape, BF16),
            vmem(w_key.shape, BF16),
            vmem((width, inner), F32),
            vmem((width, inner), F32),
            vmem((width, inner), F32),
            vmem((inner, width), F32),
            vmem(up_part.shape, BF16),
            vmem(down_part.shape, BF16),
            pltpu.SemaphoreType.DMA((7,)),
            pltpu.SemaphoreType.DMA((10,)),
        ],
        compiler_params=pltpu.CompilerParams(vmem_limit_bytes=60 * 1024 * 1024),
        name="finish",
    )(small, value_all, out_all, up_part, down_part, latents, w_query, w_key)
    return embed, level, lat, query, key, value, out, up, down


def on_device(
    pixels, w_embed, level_embed, latents, w_query, w_key, w_value, w_out, w_up, w_down, cotangent
):
    width = w_embed.shape[1]
    pooled, up_part, down_part, out_all, value_all, small = main_part(
        pixels[0], w_embed, level_embed, latents, w_query, w_key, w_value, w_out, w_up, w_down,
        cotangent.reshape(LAT * ROWS, width),
    )
    grads = finish(small, value_all, out_all, up_part, down_part, latents, w_query, w_key)
    return (pooled.reshape(LAT, ROWS, width), *grads)


def solution(mesh):
    return jax.shard_map(
        on_device,
        mesh=mesh,
        in_specs=(
            P("var", None, None, "lon"),
            *([P()] * 9),
            P(None, ("lon", "var"), None),
        ),
        out_specs=(
            P(None, ("lon", "var"), None),
            *([P()] * 7),
            P(None, "lon"),
            P("lon", None),
        ),
        check_vma=False,
    )
```

```python
import functools
import math

import jax
import jax.numpy as jnp
from jax import lax
from jax.experimental import pallas as pl
from jax.experimental.pallas import tpu as pltpu
from jax.sharding import PartitionSpec as P

F32 = jnp.float32
BF16 = jnp.bfloat16
EPSILON = 1e-05
HEADS = 16
HEAD = 64
LEV = 8
LAT = 3
ROWS = 128
TILE = 256
PAD = 128
GELU_C = math.sqrt(2.0 / math.pi)
GELU_A = 0.044715


def mm(left, right):
    return lax.dot_general(left, right, (((1,), (0,)), ((), ())), preferred_element_type=F32)


def mm_nt(left, right):
    return lax.dot_general(left, right, (((1,), (1,)), ((), ())), preferred_element_type=F32)


def mm_tn(left, right):
    return lax.dot_general(left, right, (((0,), (0,)), ((), ())), preferred_element_type=F32)


def split(value):
    high = value.astype(BF16)
    return high, (value - high.astype(F32)).astype(BF16)


def head_rows(inner):
    row = lax.broadcasted_iota(jnp.int32, (PAD, inner), 0)
    head = lax.broadcasted_iota(jnp.int32, (PAD, inner), 1) // HEAD
    return row, head


def query_rows(latents, w_query):
    queries = mm(latents, w_query).astype(BF16).astype(F32)
    inner = queries.shape[1]
    row, head = head_rows(inner)
    spread = jnp.zeros((PAD, inner), F32)
    for q in range(LAT):
        spread = jnp.where(row == q * HEADS + head, queries[q : q + 1, :], spread)
    return spread.astype(BF16)


def query_back(small_all, w_query, w_key, d_queries, d_lat):
    inner = w_key.shape[1]
    total = jnp.concatenate([small_all[0, 2 * k, 0:3].reshape(48, TILE) for k in range(2)], axis=1)
    rest = jnp.concatenate([small_all[1, 0, k] for k in range(2)], axis=1)
    spread = mm(total, w_key[...])
    row = lax.broadcasted_iota(jnp.int32, (48, inner), 0)
    head = lax.broadcasted_iota(jnp.int32, (48, inner), 1) // HEAD
    d_queries[...] = jnp.zeros_like(d_queries)
    for q in range(LAT):
        own = jnp.where(row == q * HEADS + head, spread, 0.0)
        d_queries[q : q + 1, :] = jnp.sum(own, axis=0, keepdims=True)
    high, low = split(d_queries[...])
    d_lat[...] = mm_nt(high, w_query[...]) + mm_nt(low, w_query[...]) + rest[8:16, :].astype(F32)


def prepare(latents, w_query, w_key, select, wq_high, wq_low, rows):
    inner = w_key.shape[1]
    row, head = head_rows(inner)
    for q in range(LAT):
        select[q] = jnp.where(row == q * HEADS + head, 1.0, 0.0).astype(BF16)
    spread = query_rows(latents[...], w_query[...])
    rows[...] = spread[0:48, :]
    folded = mm_nt(spread, w_key[...])
    high, low = split(folded)
    wq_high[...] = high
    wq_low[...] = low


def forward(
    px, w_embed, level_embed, w_value, wq_high, wq_low, level_rows, unit, inv, normed, normed_t, values, scores
):
    level_rows[...] = level_embed[...].astype(F32)

    @pl.loop(0, LEV, unroll=2)
    def _(l):
        token = mm_tn(px[l].reshape(80, ROWS), w_embed[...]) + level_rows[pl.ds(l, 1), :]
        token = token.astype(BF16).astype(F32)
        center = token - jnp.mean(token, axis=-1, keepdims=True)
        inverse = lax.rsqrt(jnp.mean(center * center, axis=-1, keepdims=True) + EPSILON)
        own = center * inverse
        unit[l] = own
        inv[l] = jnp.broadcast_to(inverse, (ROWS, PAD))
        own = own.astype(BF16)
        rows = pl.ds(pl.multiple_of(l * ROWS, ROWS), ROWS)
        normed[rows, :] = own
        normed_t[:, rows] = own.T
        scores[l] = (mm_nt(own, wq_high[...]) + mm_nt(own, wq_low[...])) * (1.0 / math.sqrt(HEAD))
        values[l] = mm(own, w_value[...]).astype(BF16)


def softmax(scores, weights):
    highest = scores[0]
    for l in range(1, LEV):
        highest = jnp.maximum(highest, scores[l])
    total = jnp.zeros_like(highest)
    for l in range(LEV):
        expo = jnp.exp(scores[l] - highest)
        scores[l] = expo
        total = total + expo
    for l in range(LEV):
        prob = scores[l] / total
        scores[l] = prob
        weights[l * ROWS : (l + 1) * ROWS, :] = prob.astype(BF16)


def mix(weights, select, values, spread, mixed):
    inner = values.shape[2]

    @pl.loop(0, inner // TILE)
    def _(t):
        cols = pl.ds(pl.multiple_of(t * TILE, TILE), TILE)
        for q in range(LAT):
            total = jnp.zeros((ROWS, TILE), F32)
            for l in range(LEV):
                own = mm(weights[l * ROWS : (l + 1) * ROWS, :], select[q, :, cols])
                spread[q, l, :, cols] = own.astype(BF16)
                total = total + own * values[l, :, cols].astype(F32)
            mixed[q * ROWS : (q + 1) * ROWS, cols] = total.astype(BF16)


def attend(latents, mixed, w_out, attended):
    for q in range(LAT):
        rows = slice(q * ROWS, (q + 1) * ROWS)
        own = mm(mixed[rows, :], w_out[...]) + latents[q : q + 1, :].astype(F32)
        attended[rows, :] = own.astype(BF16)


def feed_forward(attended, cot, w_up, d_hidden, d_att, hidden, d_pre):
    d_att[...] = cot[...].astype(F32)

    @pl.loop(0, w_up.shape[1] // TILE, unroll=2)
    def _(t):
        cols = pl.ds(pl.multiple_of(t * TILE, TILE), TILE)
        pre = mm(attended[...], w_up[:, cols])
        square = pre * pre
        bent = jnp.tanh(pre * (GELU_C + GELU_C * GELU_A * square))
        half = 0.5 + 0.5 * bent
        out = pre * half
        own = out.astype(BF16)
        slope = half + out * (1.0 - bent) * (GELU_C + 3.0 * GELU_C * GELU_A * square)
        back = (d_hidden[:, cols] * slope).astype(BF16)
        hidden[:, cols] = own
        d_pre[:, cols] = back
        d_att[...] += mm_nt(back, w_up[:, cols])


def value_grad(t, spread, d_mixed, normed_t, d_values):
    cols = slice(t * TILE, (t + 1) * TILE)
    for l in range(LEV):
        total = None
        for q in range(LAT):
            own = spread[q, l, :, cols] * d_mixed[q * ROWS : (q + 1) * ROWS, cols]
            total = own if total is None else total + own
        d_values[l * ROWS : (l + 1) * ROWS, cols] = total
    return mm(normed_t[...], d_values[:, cols]).astype(BF16)


def weight_grad(d_mixed, values, select, d_weights):
    d_weights[...] = jnp.zeros_like(d_weights)

    @pl.loop(0, values.shape[2] // TILE)
    def _(t):
        cols = pl.ds(pl.multiple_of(t * TILE, TILE), TILE)
        for l in range(LEV):
            own = values[l, :, cols]
            back = jnp.zeros((ROWS, PAD), F32)
            for q in range(LAT):
                d_mix = d_mixed[q * ROWS : (q + 1) * ROWS, cols]
                back = back + mm_nt(d_mix * own, select[q, :, cols])
            d_weights[l * ROWS : (l + 1) * ROWS, :] += back


def score_back(probs, d_weights, d_scores):
    total = jnp.zeros((ROWS, PAD), F32)
    for l in range(LEV):
        total = total + probs[l] * d_weights[l * ROWS : (l + 1) * ROWS, :]
    for l in range(LEV):
        rows = slice(l * ROWS, (l + 1) * ROWS)
        own = probs[l] * (d_weights[rows, :] - total) * (1.0 / math.sqrt(HEAD))
        d_scores[rows, :] = own.astype(BF16)


def token_back(levels, px, unit, inv, w_value, wq_high, d_values, d_scores, small, rest):
    for l in levels:
        rows = slice(l * ROWS, (l + 1) * ROWS)
        d_normed = mm_nt(d_values[rows, :], w_value[...]) + mm(d_scores[rows, :], wq_high[...])
        own = unit[l]
        inverse = inv[l][:, :1]
        d_token = inverse * (
            d_normed
            - jnp.mean(d_normed, axis=-1, keepdims=True)
            - own * jnp.mean(d_normed * own, axis=-1, keepdims=True)
        )
        d_token = d_token.astype(BF16)
        small[48:128, :] += mm(px[l].reshape(80, ROWS), d_token)
        rest[l : l + 1, :] = jnp.sum(d_token.astype(F32), axis=0, keepdims=True)


MESH = pl.DeviceIdType.MESH
SEMS = 160


def locate(var, lon):
    return {
        "var": var,
        "lon": lon,
        "x": lon // 4,
        "y": var % 4,
        "z": (lon // 2) % 2 * 2 + var // 4,
        "core": lon % 2,
    }


def place():
    return locate(lax.axis_index("var"), lax.axis_index("lon"))


SIZES = {"x": 4, "y": 4, "z": 4, "core": 2, "var": 8}


def peer(at, axis, index):
    var, lon = at["var"], at["lon"]
    if axis == "core":
        return var, lon - at["core"] + index
    if axis == "x":
        return var, index * 4 + lon % 4
    if axis == "y":
        return var - at["y"] + index, lon
    if axis == "z":
        return (index % 2) * 4 + at["y"], at["x"] * 4 + (index // 2) * 2 + at["core"]
    return index, lon


def greet(at):
    barrier = pltpu.get_barrier_semaphore()
    others = [peer(at, "core", 1 - at["core"])]
    steps = range(4)
    for i, j in [(i, j) for i in steps for j in steps if i or j]:
        along = locate(*peer(at, "y", (at["y"] + i) % 4))
        others.append(peer(along, "x", (at["x"] + j) % 4))
    others += [peer(at, "z", (at["z"] + i) % 4) for i in (1, 2, 3)]
    across = locate(*peer(at, "z", at["z"] + 1 - at["z"] % 2 * 2))
    others += [peer(across, "y", (at["y"] + i) % 4) for i in (1, 2, 3)]
    for other in others:
        pl.semaphore_signal(barrier, inc=1, device_id=other, device_id_type=MESH)
    pl.semaphore_wait(barrier, len(others))


class Wires:
    def __init__(self, at, send_sem, recv_sem):
        self.at, self.send_sem, self.recv_sem, self.used = at, send_sem, recv_sem, 0

    def copy(self, src, dst, device):
        slot = self.used
        self.used += 1
        return pltpu.make_async_remote_copy(
            src_ref=src,
            dst_ref=dst,
            send_sem=self.send_sem.at[slot],
            recv_sem=self.recv_sem.at[slot],
            device_id=device,
            device_id_type=MESH,
        )


HOP = 2.7
LINK = 46e3
CHIP = 500e3
ADD = 1.5 / 1024 / 2200


def size_of(ref):
    return 2 * math.prod(ref.shape)


def add_into(out, where, parts):
    if len(parts) == 2:
        out[where] = parts[0][...] + parts[1][...]
        return
    total = parts[0][...].astype(F32)
    for part in parts[1:]:
        total = total + part[...].astype(F32)
    out[where] = total.astype(BF16)


class Step:
    def __init__(self, wires, axis):
        self.wires, self.axis, self.copies = wires, axis, []
        self.hop, self.load, self.work = HOP, {}, 0.0

    def send(self, src, dst, index):
        copy = self.wires.copy(src, dst, peer(self.wires.at, self.axis, index))
        copy.start()
        self.copies.append(copy)

    def others(self):
        own, size = self.wires.at[self.axis], SIZES[self.axis]
        return [(own + d) % size for d in range(1, size)]

    def cost(self, block, parts=0):
        self.work = block / 2 * (parts + 1) * ADD if parts else 0.0
        if self.axis == "core":
            self.hop, self.load = HOP / 2, {"core": block / CHIP}
        elif self.axis == "var":
            self.load = {"y": 4 * block / LINK, "z": 4 * block / LINK}
        elif isinstance(self.axis, tuple):
            self.hop, self.load = HOP + 1.0, {axis: 8 * block / LINK for axis in self.axis}
        else:
            self.load = {self.axis: 2 * block / LINK}

    def wait(self):
        for copy in self.copies:
            copy.wait()


class Scatter(Step):
    def __init__(self, wires, axis, src, recv, out):
        super().__init__(wires, axis)
        self.src, self.recv, self.out = src, recv, out
        self.cost(size_of(out), SIZES[axis])

    def start(self):
        for d, to in enumerate(self.others()):
            self.send(self.src.at[to], self.recv.at[d], to)

    def finish(self):
        self.wait()
        own, count = self.wires.at[self.axis], len(self.copies)
        shape = self.out.shape

        def add(*index):
            refs = [self.src.at[own]] + [self.recv.at[d] for d in range(count)]
            where = index if index else (slice(None),) * len(shape)
            add_into(self.out, where, [ref.at[where] for ref in refs])

        if math.prod(shape) > 65536:

            @pl.loop(0, shape[0])
            def _(i):
                add(i, *((slice(None),) * (len(shape) - 1)))

        else:
            add()


class Total(Step):
    def __init__(self, wires, axis, src, recv, out):
        super().__init__(wires, axis)
        self.src, self.recv, self.out = src, recv, out
        self.cost(size_of(src), 4)

    def start(self):
        for d, to in enumerate(self.others()):
            self.send(self.src, self.recv.at[d], to)

    def finish(self):
        self.wait()
        add_into(self.out, ..., [self.src] + [self.recv.at[d] for d in range(len(self.copies))])


class Gather(Step):
    def __init__(self, wires, axis, full):
        super().__init__(wires, axis)
        self.full = full
        self.cost(size_of(full) // full.shape[0])

    def start(self):
        own = self.full.at[self.wires.at[self.axis]]
        for to in self.others():
            self.send(own, own, to)

    def finish(self):
        self.wait()


class Plane(Step):
    def __init__(self, wires, axes):
        super().__init__(wires, axes)

    def here(self):
        return tuple(self.wires.at[axis] for axis in self.axis)

    def others(self):
        first, second = self.here()
        ring = [(i, j) for i in range(4) for j in range(4) if i or j]
        return [((first + i) % 4, (second + j) % 4) for i, j in ring]

    def send(self, src, dst, index):
        at = dict(self.wires.at)
        for axis, place in zip(self.axis, index):
            var, lon = peer(at, axis, place)
            at = locate(var, lon)
        copy = self.wires.copy(src, dst, (var, lon))
        copy.start()
        self.copies.append(copy)


class PlaneScatter(Plane):
    def __init__(self, wires, axes, src, recv, out):
        super().__init__(wires, axes)
        self.src, self.recv, self.out = src, recv, out
        self.cost(size_of(out), 16)

    def start(self):
        for d, to in enumerate(self.others()):
            self.send(self.src.at[to], self.recv.at[d], to)

    def finish(self):
        self.wait()
        parts = [self.src.at[self.here()]] + [self.recv.at[d] for d in range(15)]
        if len(self.out.shape) == 2:
            add_into(self.out, ..., parts)
        else:
            for k in range(self.out.shape[0]):
                add_into(self.out, (k,), [part.at[k] for part in parts])


class PlaneGather(Plane):
    def __init__(self, wires, axes, full):
        super().__init__(wires, axes)
        self.full = full
        self.cost(size_of(full) // 16)

    def start(self):
        own = self.full.at[self.here()]
        for to in self.others():
            self.send(own, own, to)

    def finish(self):
        self.wait()


def ring(at, axis):
    own = at[axis]
    return own, own + 1 - 2 * (own % 2), 3 - own, (own + 2) % 4


HALVES = (slice(0, 2), slice(2, 4))


class FoldFirst(Step):
    def __init__(self, wires, axis, src, recv, out):
        super().__init__(wires, axis)
        self.src, self.recv, self.out = src, recv, out
        self.load = {axis: size_of(out) / 2 / LINK}
        self.work = size_of(out) / 2 * 3 * ADD

    def start(self):
        own, near, back, far = ring(self.wires.at, self.axis)
        for half, to in ((0, back), (1, near)):
            for slot, block in ((1, far), (0, to)):
                self.send(self.src.at[block, HALVES[half]], self.recv.at[half, slot], to)

    def finish(self):
        self.wait()
        own, near, back, far = ring(self.wires.at, self.axis)
        for half, other in ((0, near), (1, back)):
            for slot, block in ((1, other), (0, own)):
                for k in range(2):
                    add_into(
                        self.out,
                        (half, slot, k),
                        [self.src.at[block, 2 * half + k], self.recv.at[half, slot, k]],
                    )


class FoldSecond(Step):
    def __init__(self, wires, axis, src, recv, out):
        super().__init__(wires, axis)
        self.src, self.recv, self.out = src, recv, out
        self.load = {axis: size_of(out) / 2 / LINK}
        self.work = size_of(out) / 2 * 3 * ADD

    def start(self):
        own, near, back, far = ring(self.wires.at, self.axis)
        for half, to in ((0, near), (1, back)):
            self.send(self.src.at[half, 1], self.recv.at[half], to)

    def finish(self):
        self.wait()
        for half in range(2):
            add_into(self.out, (HALVES[half],), [self.src.at[half, 0], self.recv.at[half]])


class UnfoldFirst(Step):
    def __init__(self, wires, axis, full):
        super().__init__(wires, axis)
        self.full = full
        self.load = {axis: size_of(full) / 8 / LINK}

    def start(self):
        own, near, back, far = ring(self.wires.at, self.axis)
        for half, to in ((0, near), (1, back)):
            block = self.full.at[own, HALVES[half]]
            self.send(block, block, to)

    def finish(self):
        self.wait()


class UnfoldSecond(Step):
    def __init__(self, wires, axis, full):
        super().__init__(wires, axis)
        self.full = full
        self.load = {axis: size_of(full) / 4 / LINK}

    def start(self):
        own, near, back, far = ring(self.wires.at, self.axis)
        for half, other, to in ((0, near, back), (1, back, near)):
            for index in (own, other):
                block = self.full.at[index, HALVES[half]]
                self.send(block, block, to)

    def finish(self):
        self.wait()


class Chain:
    def __init__(self, steps):
        self.steps, self.next, self.after = steps, 0, None

    def advance(self):
        if self.next > 0:
            self.steps[self.next - 1].finish()
        if self.next < len(self.steps):
            self.steps[self.next].start()
        self.next += 1


class Clock:
    def __init__(self):
        self.now, self.active, self.busy = 0.0, [], {}

    def started(self, chain):
        step = chain.steps[chain.next - 1]
        ends = [self.now]
        for axis, load in step.load.items():
            self.busy[axis] = max(self.now, self.busy.get(axis, 0.0)) + load
            ends.append(self.busy[axis])
        chain.due = max(ends) + step.hop

    def begin(self, chain):
        chain.steps[0].start()
        self.begun(chain)

    def begun(self, chain):
        chain.next = 1
        self.started(chain)
        self.active.append(chain)

    def step(self, chain):
        self.now += chain.steps[chain.next - 1].work
        chain.advance()
        if chain.next > len(chain.steps):
            self.active.remove(chain)
            if chain.after is not None:
                chain.after()
        else:
            self.started(chain)

    def passed(self, time):
        self.now += time
        for chain in sorted(self.active, key=lambda chain: chain.due):
            if chain.due <= self.now:
                self.step(chain)

    def drain(self):
        while self.active:
            chain = min(self.active, key=lambda chain: chain.due)
            self.now = max(self.now, chain.due)
            self.step(chain)


class Group(Step):
    def __init__(self, steps):
        self.steps = steps
        self.hop, self.work = max(step.hop for step in steps), sum(step.work for step in steps)
        axes = {axis for step in steps for axis in step.load}
        self.load = {axis: sum(step.load.get(axis, 0.0) for step in steps) for axis in axes}

    def start(self):
        for step in self.steps:
            step.start()

    def finish(self):
        for step in self.steps:
            step.finish()


def scatter_scratch(plan, width):
    block = (16, width)
    recvs, sums, left = [pltpu.VMEM((1, 4, 4, 4, *block), BF16)], [pltpu.VMEM((4, 4, 4, *block), BF16)], 3
    for kind, _ in plan:
        if kind == "fold":
            rest = (4,) * (left - 2) + block
            recvs += [pltpu.VMEM((2, 2, 2, *rest), BF16), pltpu.VMEM((2, 2, *rest), BF16)]
            sums += [pltpu.VMEM((2, 2, 2, *rest), BF16), pltpu.VMEM((4, *rest), BF16)]
            left -= 1
        else:
            left -= 2 if kind == "plane" else 1
            rest = (4,) * left + block
            recvs.append(pltpu.VMEM((15 if kind == "plane" else 3, *rest), BF16))
            sums.append(pltpu.VMEM(rest, BF16))
    return recvs, sums[:-1]


def scatter_steps(wires, plan, src, recvs, sums, last):
    outs = [*sums, last]
    steps = [Scatter(wires, "core", src, recvs[0], outs[0])]
    for kind, axes in plan:
        kinds = {"fold": [FoldFirst, FoldSecond], "plane": [PlaneScatter], "axis": [Scatter]}[kind]
        for form in kinds:
            k = len(steps)
            steps.append(form(wires, axes, outs[k - 1], recvs[k], outs[k]))
    return steps


def plan_axes(plan):
    return [axis for kind, axes in plan for axis in (axes if kind == "plane" else (axes,))]


def whole_steps(wires, plan, src, recvs, sums, full):
    at = wires.at
    where = [at["core"], *(at[axis] for axis in plan_axes(plan))]
    steps = scatter_steps(wires, plan, src, recvs, sums, full.at[tuple(where)])
    for kind, axes in reversed(plan):
        where = where[: len(where) - (2 if kind == "plane" else 1)]
        part = full.at[tuple(where)]
        if kind == "plane":
            steps.append(PlaneGather(wires, axes, part))
        elif kind == "fold":
            steps += [UnfoldFirst(wires, axes, part), UnfoldSecond(wires, axes, part)]
        else:
            steps.append(Gather(wires, axes, part))
    return steps + [Gather(wires, "core", full)]


def part_steps(wires, plan, src, recvs, sums, full):
    last = full.at[wires.at["var"]]
    return scatter_steps(wires, plan, src, recvs, sums, last) + [Gather(wires, "var", full)]


def lock_step(*lists):
    return Chain([Group(steps) for steps in zip(*lists)])


def small_chain(wires, src, recvs, sums, full):
    core, x, y = wires.at["core"], wires.at["x"], wires.at["y"]
    return Chain([
        Scatter(wires, "core", src, recvs[0], sums[0]),
        PlaneScatter(wires, ("x", "y"), sums[0], recvs[1], sums[1]),
        Total(wires, "z", sums[1], recvs[2], full.at[core, x, y]),
        PlaneGather(wires, ("x", "y"), full.at[core]),
        Gather(wires, "core", full),
    ])


SMALL_SHAPE = (2, 4, 4, 16, TILE)


def small_scratch():
    block = SMALL_SHAPE[3:]
    recvs = [
        pltpu.VMEM((1, 4, 4, *block), BF16),
        pltpu.VMEM((15, *block), BF16),
        pltpu.VMEM((3, *block), BF16),
    ]
    sums = [pltpu.VMEM((4, 4, *block), BF16), pltpu.VMEM(block, BF16)]
    return recvs, sums


def chain_shapes(width):
    return (2, 4, 4, 4, 16, width)


WEIGHTS = 10
UP_PLAN = (("fold", "x"), ("axis", "z"), ("axis", "y"))
DOWN_PLAN = (("fold", "y"), ("axis", "z"), ("axis", "x"))
OUT_PLAN = (("axis", "z"), ("plane", ("x", "y")))
VALUE_PLAN = (("plane", ("x", "y")), ("axis", "z"))


def main_kernel(
    pixels, w_embed_h, level_embed_h, latents_h, w_query_h, w_key_h, w_value_h, w_out_h, w_up_h, w_down_h, cot_h,
    pooled, up_all, down_all, out_all, value_all, small_all, rows, d_queries, d_lat,
    loaded, work, grads, scratch, load_sem, send_sem, recv_sem,
):
    w_embed, level_embed, latents, w_query, w_key, w_value, w_out, w_up, w_down, cot, px = loaded
    (
        select, wq_high, wq_low, level_rows, unit, inv, normed, normed_t, values, scores, weights, spread, mixed,
        attended, d_att, d_att_b, d_mixed, d_values, d_weights, d_scores, hidden, d_pre, d_hidden, small, rest,
    ) = work
    up, down, out, value, small_b = grads
    at = place()
    wires = Wires(at, send_sem, recv_sem)

    pairs = [
        (latents_h, latents), (w_query_h, w_query), (w_key_h, w_key), (cot_h, cot), (w_down_h, w_down),
        (w_embed_h, w_embed), (level_embed_h, level_embed), (w_value_h, w_value), (w_out_h, w_out), (w_up_h, w_up),
    ]
    loads = [pltpu.make_async_copy(src, dst, load_sem.at[i]) for i, (src, dst) in enumerate(pairs)]
    for load in loads:
        load.start()

    def patches(index):
        return pixels.at[:, :, pl.ds(pl.multiple_of(index * ROWS, ROWS), ROWS)]

    keep = pltpu.make_async_copy(patches(at["var"]), px.at[at["var"]], load_sem.at[WEIGHTS])
    keep.start()
    greet(at)
    moves = []
    for d in range(1, 8):
        to = (at["var"] + d) % 8
        move = wires.copy(patches(to), px.at[at["var"]], peer(at, "var", to))
        move.start()
        moves.append(move)

    for load in loads[:3]:
        load.wait()
    prepare(latents, w_query, w_key, select, wq_high, wq_low, rows)
    for load in loads[3:5]:
        load.wait()

    @pl.loop(0, w_down.shape[0] // TILE, unroll=2)
    def _(t):
        cols = pl.ds(pl.multiple_of(t * TILE, TILE), TILE)
        d_hidden[:, cols] = mm_nt(cot[...], w_down[cols, :])

    for load in loads[5:8]:
        load.wait()
    keep.wait()
    for move in moves:
        move.wait()
    forward(
        px, w_embed, level_embed, w_value, wq_high, wq_low, level_rows, unit, inv, normed, normed_t, values, scores
    )
    softmax(scores, weights)
    mix(weights, select, values, spread, mixed)
    for load in loads[8:]:
        load.wait()
    attend(latents, mixed, w_out, attended)

    chain_ffn = lock_step(
        part_steps(wires, DOWN_PLAN, down, *scratch[0], down_all),
        part_steps(wires, UP_PLAN, up, *scratch[1], up_all),
    )
    chain_att = lock_step(
        whole_steps(wires, OUT_PLAN, out, *scratch[2], out_all),
        whole_steps(wires, VALUE_PLAN, value, *scratch[3], value_all),
    )
    chain_small = small_chain(wires, small_b, *scratch[4], small_all)
    clock = Clock()

    feed_forward(attended, cot, w_up, d_hidden, d_att, hidden, d_pre)
    d_att_b[...] = d_att[...].astype(BF16)
    first = chain_att.steps[0]
    for half in range(2):
        block = mm_tn(mixed[...], d_att_b[:, half * TILE : (half + 1) * TILE]).astype(BF16)
        out[half] = block.reshape(4, 4, 4, 16, TILE)
    first.steps[0].start()
    d_mixed[...] = mm_nt(d_att_b[...], w_out[...]).astype(BF16)
    for t in range(4):
        block = value_grad(t, spread, d_mixed, normed_t, d_values)
        value[t // 2, t % 2 * 2 : t % 2 * 2 + 2] = block.reshape(2, 4, 4, 16, TILE)
    first.steps[1].start()
    clock.begun(chain_att)
    for t in range(8):
        cols = slice(t * TILE, (t + 1) * TILE)
        x, z_hi = t // 2, t % 2
        block = mm_tn(hidden[:, cols], cot[...]).astype(BF16)
        other = mm_tn(d_pre[:, cols], attended[...]).astype(BF16)
        for core in range(2):
            for var in range(8):
                z, y = z_hi * 2 + var // 4, var % 4
                start = core * 128 + var * 16
                down[core, y, z, x] = block[start : start + 16]
                up[core, x, z, y] = other[start : start + 16]
        clock.passed(0.5)
    clock.begin(chain_ffn)
    for q in range(LAT):
        rows = slice(q * ROWS, (q + 1) * ROWS)
        pooled[rows, :] = (attended[rows, :].astype(F32) + mm(hidden[rows, :], w_down[...])).astype(BF16)
    clock.passed(1.0)
    weight_grad(d_mixed, values, select, d_weights)
    clock.passed(2.5)
    score_back(scores, d_weights, d_scores)
    clock.passed(0.5)
    small[...] = jnp.zeros_like(small)
    rest[...] = jnp.zeros_like(rest)
    for l in range(0, LEV, 2):
        token_back((l, l + 1), px, unit, inv, w_value, wq_high, d_values, d_scores, small, rest)
        clock.passed(1.7)
    small[0:48, :] = mm_tn(d_scores[...], normed[...])[0:48, :]
    for q in range(LAT):
        rest[8 + q : 9 + q, :] = jnp.sum(d_att[q * ROWS : (q + 1) * ROWS, :], axis=0, keepdims=True)
    small_b[...] = jnp.zeros_like(small_b)
    for k in range(2):
        cols = slice(k * TILE, (k + 1) * TILE)
        small_b[0, 2 * k : 2 * k + 2] = small[:, cols].astype(BF16).reshape(2, 4, 16, TILE)
        small_b[1, 0, k] = rest[:, cols].astype(BF16)
    clock.passed(0.5)
    chain_small.after = lambda: query_back(small_all, w_query, w_key, d_queries, d_lat)
    clock.begin(chain_small)
    clock.drain()


def main_part(pixels, w_embed, level_embed, latents, w_query, w_key, w_value, w_out, w_up, w_down, cot):
    width, inner = w_key.shape
    every, pairs = LEV * ROWS, LAT * ROWS
    shape = jax.ShapeDtypeStruct
    whole = pl.BlockSpec(memory_space=pltpu.VMEM)
    vmem = pltpu.VMEM
    arrays = (w_embed, level_embed, latents, w_query, w_key, w_value, w_out, w_up, w_down, cot)
    loaded = [vmem(array.shape, BF16) for array in arrays] + [vmem((LEV, 5, 16, ROWS), BF16)]
    work = [
        vmem((LAT, PAD, inner), BF16),
        vmem((PAD, width), BF16),
        vmem((PAD, width), BF16),
        vmem((LEV, width), F32),
        vmem((LEV, ROWS, width), F32),
        vmem((LEV, ROWS, PAD), F32),
        vmem((every, width), BF16),
        vmem((width, every), BF16),
        vmem((LEV, ROWS, inner), BF16),
        vmem((LEV, ROWS, PAD), F32),
        vmem((every, PAD), BF16),
        vmem((LAT, LEV, ROWS, inner), BF16),
        vmem((pairs, inner), BF16),
        vmem((pairs, width), BF16),
        vmem((pairs, width), F32),
        vmem((pairs, width), BF16),
        vmem((pairs, inner), BF16),
        vmem((every, inner), BF16),
        vmem((every, PAD), F32),
        vmem((every, PAD), BF16),
        vmem((pairs, w_up.shape[1]), BF16),
        vmem((pairs, w_up.shape[1]), BF16),
        vmem((pairs, w_up.shape[1]), F32),
        vmem((128, width), F32),
        vmem((16, width), F32),
    ]
    grads = [
        vmem(chain_shapes(width), BF16),
        vmem(chain_shapes(width), BF16),
        vmem(chain_shapes(TILE), BF16),
        vmem(chain_shapes(TILE), BF16),
        vmem(SMALL_SHAPE, BF16),
    ]
    return pl.pallas_call(
        main_kernel,
        out_shape=(
            shape((pairs, width), BF16),
            shape((8, 16, width), BF16),
            shape((8, 16, width), BF16),
            shape(chain_shapes(TILE), BF16),
            shape(chain_shapes(TILE), BF16),
            shape(SMALL_SHAPE, BF16),
            shape((48, inner), BF16),
            shape((8, inner), F32),
            shape((8, width), F32),
        ),
        in_specs=[pl.BlockSpec(memory_space=pl.ANY)] * 11,
        out_specs=(whole,) * 9,
        scratch_shapes=[
            loaded,
            work,
            grads,
            [
                scatter_scratch(DOWN_PLAN, width),
                scatter_scratch(UP_PLAN, width),
                scatter_scratch(OUT_PLAN, TILE),
                scatter_scratch(VALUE_PLAN, TILE),
                small_scratch(),
            ],
            pltpu.SemaphoreType.DMA((WEIGHTS + 1,)),
            pltpu.SemaphoreType.DMA((SEMS,)),
            pltpu.SemaphoreType.DMA((SEMS,)),
        ],
        compiler_params=pltpu.CompilerParams(
            vmem_limit_bytes=60 * 1024 * 1024, collective_id=0, has_side_effects=True
        ),
        name="main_part",
    )(pixels, w_embed, level_embed, latents, w_query, w_key, w_value, w_out, w_up, w_down, cot)


def finish_kernel(
    small_h, rows_h, queries_h, value_h, out_h, up_h, down_h, pooled_h, d_lat, latents,
    grad_embed, grad_level, grad_lat, grad_up, grad_down, query_h, key_h, value_g, out_g, pooled_g,
    small, rows, d_queries, value_all, out_all, up_part, down_part,
    grad_query, grad_key, grad_value, grad_out, load_sem, save_sem,
):
    pairs = [
        (small_h, small), (rows_h, rows), (queries_h, d_queries), (value_h, value_all), (out_h, out_all),
        (up_h, up_part), (down_h, down_part),
    ]
    loads = [pltpu.make_async_copy(src, dst, load_sem.at[i]) for i, (src, dst) in enumerate(pairs)]
    for load in loads:
        load.start()
    saves = []

    def save(src, dst):
        copy = pltpu.make_async_copy(src, dst, save_sem.at[len(saves)])
        copy.start()
        saves.append(copy)

    width, inner = grad_key.shape
    save(pooled_h, pooled_g)
    for load in loads[0:3]:
        load.wait()
    sums = jnp.concatenate([small[0, 2 * k : 2 * k + 2].reshape(128, TILE) for k in range(2)], axis=1)
    rest = jnp.concatenate([small[1, 0, k] for k in range(2)], axis=1)
    total = sums[0:48, :]
    for t in range(2):
        cols = slice(t * 512, (t + 1) * 512)
        grad_key[:, cols] = mm_tn(total, rows[:, cols])
        save(grad_key.at[:, cols], key_h.at[:, cols])
    high, low = split(d_queries[0:LAT, :])
    for t in range(2):
        cols = slice(t * 512, (t + 1) * 512)
        grad_query[:, cols] = mm_tn(latents[...], high[:, cols]) + mm_tn(latents[...], low[:, cols])
        save(grad_query.at[:, cols], query_h.at[:, cols])
    loads[3].wait()
    for t in range(4):
        block = value_all[t // 2, t % 2 * 2 : t % 2 * 2 + 2].reshape(width, TILE)
        cols = slice(t * TILE, (t + 1) * TILE)
        grad_value[:, cols] = block.astype(F32)
        save(grad_value.at[:, cols], value_g.at[:, cols])
    loads[4].wait()
    for half in range(2):
        cols = slice(half * TILE, (half + 1) * TILE)
        grad_out[:, cols] = out_all[half].reshape(inner, TILE).astype(F32)
        save(grad_out.at[:, cols], out_g.at[:, cols])
    grad_lat[...] = d_lat[0:LAT, :]
    grad_embed[...] = sums[48:128, :].astype(F32)
    grad_level[...] = rest[0:8, :].astype(F32)
    for load in loads[5:]:
        load.wait()
    grad_up[...] = up_part[...].reshape(ROWS, -1).astype(F32).T
    grad_down[...] = down_part[...].reshape(ROWS, -1).astype(F32)
    for copy in saves:
        copy.wait()


def finish(small, rows, d_queries, value_all, out_all, up_part, down_part, pooled, d_lat, latents):
    width, inner = latents.shape[1], rows.shape[1]
    shape = jax.ShapeDtypeStruct
    whole = pl.BlockSpec(memory_space=pltpu.VMEM)
    anywhere = pl.BlockSpec(memory_space=pl.ANY)
    vmem = pltpu.VMEM
    loaded = (small, rows, d_queries, value_all, out_all, up_part, down_part)
    embed, level, lat, up, down, query, key, value, out, pooled = pl.pallas_call(
        finish_kernel,
        out_shape=(
            shape((80, width), F32),
            shape((LEV, width), F32),
            shape((LAT, width), F32),
            shape((width, ROWS), F32),
            shape((ROWS, width), F32),
            shape((width, inner), F32),
            shape((width, inner), F32),
            shape((width, inner), F32),
            shape((inner, width), F32),
            shape(pooled.shape, BF16),
        ),
        in_specs=[anywhere] * 8 + [whole] * 2,
        out_specs=(whole,) * 5 + (anywhere,) * 5,
        scratch_shapes=[vmem(array.shape, array.dtype) for array in loaded]
        + [
            vmem((width, inner), F32),
            vmem((width, inner), F32),
            vmem((width, inner), F32),
            vmem((inner, width), F32),
            pltpu.SemaphoreType.DMA((7,)),
            pltpu.SemaphoreType.DMA((11,)),
        ],
        compiler_params=pltpu.CompilerParams(vmem_limit_bytes=60 * 1024 * 1024),
        name="finish",
    )(*loaded, pooled, d_lat, latents)
    return pooled, embed, level, lat, query, key, value, out, up, down


def on_device(
    pixels, w_embed, level_embed, latents, w_query, w_key, w_value, w_out, w_up, w_down, cotangent
):
    width = w_embed.shape[1]
    pooled, up_part, down_part, out_all, value_all, small, rows, d_queries, d_lat = main_part(
        pixels[0], w_embed, level_embed, latents, w_query, w_key, w_value, w_out, w_up, w_down,
        cotangent.reshape(LAT * ROWS, width),
    )
    pooled, *grads = finish(
        small, rows, d_queries, value_all, out_all, up_part, down_part, pooled, d_lat, latents
    )
    return (pooled.reshape(LAT, ROWS, width), *grads)


def solution(mesh):
    return jax.shard_map(
        on_device,
        mesh=mesh,
        in_specs=(
            P("var", None, None, "lon"),
            *([P()] * 9),
            P(None, ("lon", "var"), None),
        ),
        out_specs=(
            P(None, ("lon", "var"), None),
            *([P()] * 7),
            P(None, "lon"),
            P("lon", None),
        ),
        check_vma=False,
    )
```
